32 devices in a mesh: view: 2 (over x), gz: 16 (over z, y, core).
Axes of the slice: x: 2, y: 2, z: 4, core: 2. Of those that a mesh axis runs over, the one named last changes fastest.
Arguments:
- estimate: float32 [512, 128, 128], P('gz'), may hold values from 0.25 to 4
- raw_bricks: bfloat16 [2, 8192, 4, 2, 128], P('view', 'gz'), may hold values from 0.25 to 4
- brick_slab: int32 [2, 8192, 1], P('view', 'gz'), may hold values from 0 to 15; in each aligned block of 512 rows (0 to 511, 512 to 1023, ..., all dimensions but the last counted through in order) at most 64 rows name the same one
- brick_pos: int32 [2, 8192], P('view', 'gz'), may hold values from 0 to 511
- off_z: int32 [2, 4], P('view'), may hold values from -1 to 3
- frac_z: float32 [2, 4], P('view'), may hold values from 0 to 1
- off_y: int32 [2, 2], P('view'), may hold values from -1 to 1
- frac_y: float32 [2, 2], P('view'), may hold values from 0 to 1
- off_x: int32 [2, 128], P('view'), may hold values from -1 to 127
- frac_x: float32 [2, 128], P('view'), may hold values from 0 to 1
- psf_z: float32 [2, 64], P('view'), may hold values from 0.05 to 1
- psf_y: float32 [2, 16], P('view'), may hold values from 0.05 to 1
- psf_x: float32 [2, 16], P('view'), may hold values from 0.05 to 1
Outputs:
- new_estimate: float32 [512, 128, 128], P('gz', 'view')
The draws below stay inside these ranges and needn't reach their ends.
Inputs may be any that keep to these rules, and one draw needn't show every extreme that they name: `brick_slab`: in every view, the 512 bricks held by one device (an aligned block) name any one slab at most 64 times, a bound that some block reaches.
All inputs are finite; a program needn't handle non-finite values.
Results may differ from the reference program's by a relative error of at most 0.00043.
Values may be sent and summed in bfloat16 or wider, within the bound.
A program may use at most 64 MiB of HBM per device.

```python
import math
import jax
import jax.numpy as jnp
import numpy as np
from jax import lax

CZ = 32
NY = 128
NX = 128
KZ = 64
KXY = 16
BZ = 4
BY = 2
VIEWS = 2
NZ = 512
BPD = 512
BRICKS = 8192
CAP = 64
POS = 512
N_GZ = 16


def place_ends(entries, key, low, high):
    spot = [jax.random.randint(jax.random.fold_in(key, axis), (), 0, length) for axis, length in enumerate(entries.shape)]
    main_axis = entries.shape.index(max(entries.shape))
    beside = spot[:main_axis] + [(spot[main_axis] + 1) % entries.shape[main_axis]] + spot[main_axis + 1:]
    return entries.at[tuple(spot)].set(low).at[tuple(beside)].set(high)


def block_levels(stream_key, dims, cuts, smallest, high):
    level = 1.0
    for axis_at, parts in cuts:
        heights = jax.random.uniform(jax.random.fold_in(jax.random.fold_in(stream_key, 6), axis_at), (parts,), jnp.float32, smallest / len(cuts), high / len(cuts))
        level = level * jnp.repeat(jnp.exp(heights), dims[axis_at] // parts).reshape((-1,) + (1,) * (len(dims) - 1 - axis_at))
    return level


def deal_out(stream_key, own, number, rows, amount, top, reach, skew):
    sequence = jax.random.permutation(stream_key, amount)
    packed, usual = shares(amount, rows * top, reach, skew, True), shares(amount, rows * top, reach, skew, False)
    places = jnp.arange(amount)

    def named(tallies, rotation):
        used = int((tallies > 0).sum())
        fixed = max(1, used // 4)
        moved = fixed + (places - fixed + rotation * (used - fixed)) % max(1, amount - fixed)
        return jnp.zeros((amount,), jnp.int32).at[sequence[jnp.where(places < fixed, places, moved)]].set(jnp.asarray(tallies, jnp.int32))

    tallies = jnp.where(number % 4 == 0, named(packed, number // 4), named(usual, number - number // 4 - 1))
    mixed = jax.random.permutation(jax.random.fold_in(own, 3), amount)
    giver, sink = mixed[0:amount // 2 * 2:2], mixed[1:amount // 2 * 2:2]
    margin = jnp.minimum(tallies[giver] - 1, reach - tallies[sink]) // 2
    margin = jnp.where((giver == sequence[0]) | (sink == sequence[0]) | (tallies[sink] == 0), 0, jnp.maximum(margin, 0))
    moved = jax.random.randint(jax.random.fold_in(own, 4), (amount // 2,), 0, 1 << 20) % (margin + 1)
    tallies = tallies.at[giver].add(-moved).at[sink].add(moved)
    labels = jnp.searchsorted(jnp.cumsum(tallies), jnp.arange(rows * top), side="right").astype(jnp.int32)
    grid = labels.reshape(top, rows).T
    grid = grid[jax.random.permutation(jax.random.fold_in(own, 1), rows)]
    rotation = jax.random.randint(jax.random.fold_in(own, 2), (rows, 1), 0, top)
    return jnp.take_along_axis(grid, (jnp.arange(top)[None, :] + rotation) % top, axis=1)


def shares(number_of, total, reach, lean, full):
    loads = [(1 << 20) // math.isqrt(standing ** lean) + 1 for standing in range(1, number_of + 1)]
    largest = reach if full else min(reach, max(-(-total // number_of), total * loads[0] // sum(loads)))
    least = 1 if total - largest >= number_of - 1 else 0
    holding, rest = [largest] + [least] * (number_of - 1), total - largest - least * (number_of - 1)
    while rest > 0:
        free = [i for i in range(1, number_of) if holding[i] < largest] or [i for i in range(1, number_of) if holding[i] < reach]
        mass, budget = sum([loads[i] for i in free]), rest
        for i in free:
            extra = min(reach - holding[i], max(1, budget * loads[i] // mass), rest)
            holding[i] = holding[i] + extra
            rest = rest - extra
    return np.array(holding)


def setup_inputs(seed: int = 0) -> dict:
    splits = jax.random.split(jax.random.key(seed), 14)
    estimate = jnp.clip(jnp.exp(math.log(4.0) - 2.7725887 * jax.random.uniform(splits[0], (NZ, NY, NX), jnp.float32) ** block_levels(splits[0], (NZ, NY, NX), ((0, 16),), -0.2, 0.2)), 0.25, 4.0)
    raw_bricks = jnp.clip(jnp.exp(math.log(4.0) - 2.7725887 * jax.random.uniform(splits[1], (VIEWS, BRICKS, BZ, BY, NX), jnp.float32) ** block_levels(splits[1], (VIEWS, BRICKS, BZ, BY, NX), ((0, 2), (1, 16)), -0.2, 0.2)), 0.25, 4.0).astype(jnp.bfloat16)
    brick_slab_keys = jax.random.split(jax.random.fold_in(splits[2], 1), VIEWS * BRICKS // BPD)
    brick_slab_turns = jax.random.permutation(jax.random.fold_in(splits[2], 3), VIEWS * BRICKS // BPD)
    brick_slab = jax.vmap(lambda own, number: deal_out(jax.random.fold_in(splits[2], 2), own, number, BPD, N_GZ, 1, CAP, 2))(brick_slab_keys, brick_slab_turns).reshape((VIEWS, BRICKS, 1))
    brick_pos = place_ends(jax.random.randint(splits[3], (VIEWS, BRICKS), 0, POS), jax.random.fold_in(splits[3], 1), 0, POS - 1).astype(jnp.int32)
    off_z = place_ends(jax.random.randint(splits[4], (VIEWS, BZ), -1, BZ), jax.random.fold_in(splits[4], 1), -1, BZ - 1).astype(jnp.int32)
    frac_z = jnp.clip(1.0 * jax.random.uniform(splits[5], (VIEWS, BZ), jnp.float32) ** block_levels(splits[5], (VIEWS, BZ), ((0, 2),), -0.2, 0.2), 0.0, 1.0)
    off_y = place_ends(jax.random.randint(splits[6], (VIEWS, BY), -1, BY), jax.random.fold_in(splits[6], 1), -1, BY - 1).astype(jnp.int32)
    frac_y = jnp.clip(1.0 * jax.random.uniform(splits[7], (VIEWS, BY), jnp.float32) ** block_levels(splits[7], (VIEWS, BY), ((0, 2),), -0.2, 0.2), 0.0, 1.0)
    off_x = place_ends(jax.random.randint(splits[8], (VIEWS, NX), -1, NX), jax.random.fold_in(splits[8], 1), -1, NX - 1).astype(jnp.int32)
    frac_x = jnp.clip(1.0 * jax.random.uniform(splits[9], (VIEWS, NX), jnp.float32) ** block_levels(splits[9], (VIEWS, NX), ((0, 2),), -0.2, 0.2), 0.0, 1.0)
    psf_z = jnp.clip(jnp.exp(math.log(1.0) - 2.9957323 * jax.random.uniform(splits[10], (VIEWS, KZ), jnp.float32) ** block_levels(splits[10], (VIEWS, KZ), ((0, 2),), -0.2, 0.2)), 0.05, 1.0)
    psf_y = jnp.clip(jnp.exp(math.log(1.0) - 2.9957323 * jax.random.uniform(splits[11], (VIEWS, KXY), jnp.float32) ** block_levels(splits[11], (VIEWS, KXY), ((0, 2),), -0.2, 0.2)), 0.05, 1.0)
    psf_x = jnp.clip(jnp.exp(math.log(1.0) - 2.9957323 * jax.random.uniform(splits[12], (VIEWS, KXY), jnp.float32) ** block_levels(splits[12], (VIEWS, KXY), ((0, 2),), -0.2, 0.2)), 0.05, 1.0)
    return dict(estimate=estimate, raw_bricks=raw_bricks, brick_slab=brick_slab, brick_pos=brick_pos, off_z=off_z, frac_z=frac_z, off_y=off_y, frac_y=frac_y, off_x=off_x, frac_x=frac_x, psf_z=psf_z, psf_y=psf_y, psf_x=psf_x)


def rounded(values):
    return lax.optimization_barrier(values.astype(jnp.bfloat16)).astype(jnp.float32)


def weight_table(offsets, fractions, length):
    source_rows = jnp.arange(length, dtype=jnp.int32)[:, None]
    low_weight = rounded(1.0 - fractions)[None, :]
    high_weight = rounded(fractions)[None, :]
    table = jnp.where(source_rows == offsets[None, :], low_weight, jnp.float32(0.0))
    return table + jnp.where(source_rows == offsets[None, :] + 1, high_weight, jnp.float32(0.0))


def shifted_sum(padded, taps, axis, starts, length):
    result = None
    for tap_index in range(len(starts)):
        piece = taps[tap_index] * lax.slice_in_dim(padded, starts[tap_index], starts[tap_index] + length, axis=axis)
        result = piece if result is None else result + piece
    return result


def reference(estimate, raw_bricks, brick_slab, brick_pos, off_z, frac_z, off_y, frac_y, off_x, frac_x, psf_z, psf_y, psf_x):
    estimate_b = rounded(estimate)
    block_rows = NY // BY
    half_z = KZ // 2
    half_lat = KXY // 2

    def add_view(view, running):
        bricks = raw_bricks[view].astype(jnp.float32)
        offsets_x = off_x[view]
        fractions_x = frac_x[view]
        padded_x = jnp.pad(bricks, ((0, 0), (0, 0), (0, 0), (1, 1)))
        along_x = rounded(1.0 - fractions_x) * jnp.take(padded_x, offsets_x + 1, axis=3)
        along_x = along_x + rounded(fractions_x) * jnp.take(padded_x, offsets_x + 2, axis=3)
        along_x = rounded(along_x)
        table_z = weight_table(off_z[view], frac_z[view], BZ)
        table_y = weight_table(off_y[view], frac_y[view], BY)
        table_zy = rounded(jnp.einsum("ac,bd->abcd", table_z, table_y).reshape(BZ * BY, BZ * BY))
        mixed = jnp.einsum("qp,nqx->npx", table_zy, along_x.reshape(BRICKS, BZ * BY, NX))
        mixed = rounded(mixed)
        slab_ids = brick_slab[view, :, 0]
        places = brick_pos[view]
        block_z = (slab_ids * (CZ // BZ) + places // block_rows).astype(jnp.int32)
        block_y = (places % block_rows).astype(jnp.int32)
        blocks = jnp.zeros((NZ // BZ, block_rows, BZ, BY, NX), jnp.float32)
        blocks = blocks.at[block_z, block_y].add(mixed.reshape(BRICKS, BZ, BY, NX))
        joined = 1.0 + blocks.transpose(0, 2, 1, 3, 4).reshape(NZ, NY, NX)
        taps_z = rounded(psf_z[view] / jnp.sum(psf_z[view]))
        taps_y = rounded(psf_y[view] / jnp.sum(psf_y[view]))
        taps_x = rounded(psf_x[view] / jnp.sum(psf_x[view]))
        padded = jnp.pad(estimate_b, ((half_z, half_z), (0, 0), (0, 0)))
        blur_z = rounded(shifted_sum(padded, taps_z, 0, list(range(KZ)), NZ))
        padded = jnp.pad(blur_z, ((0, 0), (half_lat, KXY - 1 - half_lat), (0, 0)))
        blur_y = rounded(shifted_sum(padded, taps_y, 1, list(range(KXY)), NY))
        padded = jnp.pad(blur_y, ((0, 0), (0, 0), (half_lat, KXY - 1 - half_lat)))
        blurred = shifted_sum(padded, taps_x, 2, list(range(KXY)), NX)
        ratio = rounded(joined / blurred)
        padded = jnp.pad(ratio, ((half_z, half_z), (0, 0), (0, 0)))
        back_z = rounded(shifted_sum(padded, taps_z, 0, [2 * half_z - tap_index for tap_index in range(KZ)], NZ))
        padded = jnp.pad(back_z, ((0, 0), (KXY - 1 - half_lat, half_lat), (0, 0)))
        back_y = rounded(shifted_sum(padded, taps_y, 1, [KXY - 1 - tap_index for tap_index in range(KXY)], NY))
        padded = jnp.pad(back_y, ((0, 0), (0, 0), (KXY - 1 - half_lat, half_lat)))
        correction = shifted_sum(padded, taps_x, 2, [KXY - 1 - tap_index for tap_index in range(KXY)], NX)
        return running + correction

    total = lax.fori_loop(0, VIEWS, add_view, jnp.zeros((NZ, NY, NX), jnp.float32))
    return estimate * total / VIEWS
```

```python
import functools

import jax
import jax.numpy as jnp
from jax import lax
from jax.experimental import pallas as pl
from jax.experimental.pallas import tpu as pltpu
from jax.sharding import PartitionSpec as P

BF16 = jnp.bfloat16
F32 = jnp.float32
CHUNKS = 4


def iota(shape, dim):
    return lax.broadcasted_iota(jnp.int32, shape, dim)


def tap_table(psf, count, which):
    total = psf[0, 0]
    for k in range(1, count):
        total = total + psf[0, k]
    table = jnp.zeros(which.shape, F32)
    for k in range(count):
        table = jnp.where(which == k, psf[0, k], table)
    return (table / jnp.full(which.shape, total, F32)).astype(BF16)


def small_weight(off, frac, column, source):
    fraction = jnp.full((1, 128), frac[0, column], F32)
    offset = jnp.full((1, 128), off[0, column], jnp.int32)
    low = (1.0 - fraction).astype(BF16).astype(F32)
    high = fraction.astype(BF16).astype(F32)
    return jnp.where(offset == source, low, 0.0) + jnp.where(offset + 1 == source, high, 0.0)


def step(
    dims,
    est, raw, slab, pos, off_z, frac_z, off_y, frac_y, off_x, frac_x, psf_z, psf_y, psf_x,
    out,
    pad1, pad2, work, blurred, joined, weights, mixed, outgoing, arrived, pos_out, pos_in, pos_row,
    placer, back, from_views, x_tables, slot_scr,
    halo_send, halo_recv, brick_send, brick_recv, pos_send, pos_recv, view_send, view_recv,
    xt_send, xt_recv, own_sem,
):
    planes, rows, cols, depth, height, bricks, n, nv, taps_z, taps_l = dims
    cells = depth * height
    wide = cells * cols
    cap = max(2, 2 * bricks // n)
    slots = n * cap
    block_planes = planes // depth
    block_rows = rows // height
    places = block_planes * block_rows
    half = taps_z // 2
    lat = taps_l // 2
    share = rows // nv
    part = rows // CHUNKS
    zpart = planes // CHUNKS
    me = lax.axis_index("gz")
    mv = lax.axis_index("view")

    barrier = pltpu.get_barrier_semaphore()

    @pl.loop(1, n)
    def _(i):
        pl.semaphore_signal(barrier, inc=1, device_id={"gz": lax.rem(me + i, n)})

    @pl.loop(1, nv)
    def _(i):
        pl.semaphore_signal(barrier, inc=1, device_id={"view": lax.rem(mv + i, nv)})

    def own_rows(source, pad):
        @pl.loop(0, rows, unroll=4)
        def _(y):
            pad[y, pl.ds(planes, planes), :] = source[pl.ds(y, planes, stride=rows), :].astype(BF16)

    own_rows(est, pad1)

    pl.semaphore_wait(barrier, n - 1 + nv - 1)

    def halo(pad, phase, to_right, c):
        peer = lax.rem(me + 1, n) if to_right else lax.rem(me + n - 1, n)
        side = 0 if to_right else 1
        return pltpu.make_async_remote_copy(
            src_ref=pad.at[pl.ds(c * part, part), pl.ds(planes, planes), :],
            dst_ref=pad.at[pl.ds(c * part, part), pl.ds(0 if to_right else 2 * planes, planes), :],
            send_sem=halo_send.at[phase, side, c],
            recv_sem=halo_recv.at[phase, side, c],
            device_id={"gz": peer},
            device_id_type=pl.DeviceIdType.MESH,
        )

    def halo_start(pad, phase, c):
        @pl.when(me < n - 1)
        def _():
            halo(pad, phase, True, c).start()

        @pl.when(me > 0)
        def _():
            halo(pad, phase, False, c).start()

    def halo_wait(pad, phase, c):
        @pl.when(me > 0)
        def _():
            halo(pad, phase, True, c).wait_recv()

        @pl.when(me < n - 1)
        def _():
            halo(pad, phase, False, c).wait_recv()

    def halo_sent(pad, phase, c):
        @pl.when(me < n - 1)
        def _():
            halo(pad, phase, True, c).wait_send()

        @pl.when(me > 0)
        def _():
            halo(pad, phase, False, c).wait_send()

    for c in range(CHUNKS):
        halo_start(pad1, 0, c)

    @pl.when(me == 0)
    def _():
        for pad in (pad1, pad2):
            pad[:, pl.ds(0, planes), :] = jnp.zeros((rows, planes, cols), BF16)

    @pl.when(me == n - 1)
    def _():
        for pad in (pad1, pad2):
            pad[:, pl.ds(2 * planes, planes), :] = jnp.zeros((rows, planes, cols), BF16)

    source = iota((cols, cols), 0)
    low = (1.0 - frac_x[...]).astype(BF16).astype(F32)
    high = frac_x[...].astype(BF16).astype(F32)
    along = jnp.where(source == off_x[...], low, 0.0) + jnp.where(source == off_x[...] + 1, high, 0.0)
    for a in range(depth):
        for c in range(depth):
            wz = small_weight(off_z, frac_z, c, a)
            for e in range(height):
                for d in range(height):
                    wy = small_weight(off_y, frac_y, d, e)
                    wzy = (wz * wy).astype(BF16).astype(F32)
                    weights[
                        (a * height + e) * cols:(a * height + e + 1) * cols,
                        (c * height + d) * cols:(c * height + d + 1) * cols,
                    ] = (along * wzy).astype(BF16)
    for i in range(wide // 256):
        mixed[:, i * 256:(i + 1) * 256] = jnp.dot(
            raw[...], weights[:, i * 256:(i + 1) * 256], preferred_element_type=F32
        ).astype(BF16)

    slab_v = slab[...]
    member = iota((n, bricks), 0) == slab_v
    before = (iota((bricks, bricks), 0) < iota((bricks, bricks), 1)).astype(F32).astype(BF16)
    earlier = jnp.dot(member.astype(F32).astype(BF16), before, preferred_element_type=F32)
    order = jnp.sum(jnp.where(member, earlier, 0.0), axis=0, keepdims=True).astype(jnp.int32)
    slot_scr[...] = slab_v * cap + order
    pos_v = pos[...]
    row16 = iota((16, bricks), 0)
    pos_pair = jnp.where(
        row16 == 0, pos_v // 64 + 1, jnp.where(row16 == 1, lax.rem(pos_v, 64), 0)
    ).astype(F32).astype(BF16)
    for i in range(slots // 256):
        chosen = ((iota((256, bricks), 0) + i * 256) == slot_scr[...]).astype(F32).astype(BF16)
        outgoing[i * 256:(i + 1) * 256, :] = jnp.dot(
            chosen, mixed[...], preferred_element_type=F32
        ).astype(BF16)
        slot_pos = lax.dot_general(
            pos_pair, chosen, (((1,), (1,)), ((), ())), preferred_element_type=F32
        )
        for j in range(256 // cap):
            pos_out[i * (256 // cap) + j, :, 0:cap] = slot_pos[:, j * cap:(j + 1) * cap].astype(BF16)

    def brick_copy(peer, owner):
        return pltpu.make_async_remote_copy(
            src_ref=outgoing.at[pl.ds(pl.multiple_of(peer * cap, cap), cap), :],
            dst_ref=arrived.at[pl.ds(pl.multiple_of(owner * cap, cap), cap), :],
            send_sem=brick_send.at[peer],
            recv_sem=brick_recv.at[owner],
            device_id={"gz": peer},
            device_id_type=pl.DeviceIdType.MESH,
        )

    def pos_copy(peer, owner):
        return pltpu.make_async_remote_copy(
            src_ref=pos_out.at[peer],
            dst_ref=pos_in.at[owner],
            send_sem=pos_send.at[peer],
            recv_sem=pos_recv.at[owner],
            device_id={"gz": peer},
            device_id_type=pl.DeviceIdType.MESH,
        )

    @pl.loop(1, n)
    def _(i):
        peer = lax.rem(me + i, n)
        brick_copy(peer, me).start()
        pos_copy(peer, me).start()

    mine = pl.ds(pl.multiple_of(me * cap, cap), cap)
    own_bricks = pltpu.make_async_copy(outgoing.at[mine, :], arrived.at[mine, :], own_sem.at[0])
    own_pos = pltpu.make_async_copy(pos_out.at[me], pos_in.at[me], own_sem.at[1])
    own_bricks.start()
    own_pos.start()

    def true_row(r):
        return lax.rem(r, block_rows) * height + r // block_rows

    ii, jj = iota((rows, rows), 0), iota((rows, rows), 1)
    fy = tap_table(psf_y, taps_l, jj - true_row(ii) + lat)
    by = tap_table(psf_y, taps_l, ii - true_row(jj) + lat)
    ci, cj = iota((cols, cols), 0), iota((cols, cols), 1)
    fx = tap_table(psf_x, taps_l, ci - cj + lat)
    x_tables[mv] = tap_table(psf_x, taps_l, cj - ci + lat)
    zi, zj = iota((planes, 3 * planes), 0), iota((planes, 3 * planes), 1)
    fz = tap_table(psf_z, taps_z, zj - zi - (planes - half))
    bz = tap_table(psf_z, taps_z, planes + half + zi - zj)

    def xt_copy(peer, owner):
        return pltpu.make_async_remote_copy(
            src_ref=x_tables.at[mv],
            dst_ref=x_tables.at[owner],
            send_sem=xt_send.at[peer],
            recv_sem=xt_recv.at[owner],
            device_id={"view": peer},
            device_id_type=pl.DeviceIdType.MESH,
        )

    @pl.loop(1, nv)
    def _(i):
        xt_copy(lax.rem(mv + i, nv), mv).start()

    def z_pass(pad, table, c):
        @pl.loop(0, part // 4, unroll=2)
        def _(i):
            y = c * part + i * 4
            block = jnp.concatenate([pad[y + j] for j in range(4)], axis=1)
            result = jnp.dot(table, block, preferred_element_type=F32)
            result = result.astype(BF16).astype(F32)
            for j in range(4):
                work[pl.ds((y + j) * planes, planes), :] = result[:, j * cols:(j + 1) * cols]

    def y_pass(table, z):
        block = jnp.concatenate(
            [work[pl.ds(z + j, rows, stride=planes), :].astype(BF16) for j in range(2)], axis=1
        )
        return jnp.dot(table, block, preferred_element_type=F32).astype(BF16)

    for c in range(CHUNKS):
        halo_wait(pad1, 0, c)
        z_pass(pad1, fz, c)

    @pl.loop(0, planes // 2, unroll=2)
    def _(i):
        along_y = y_pass(fy, 2 * i)
        for j in range(2):
            blurred[2 * i + j] = jnp.dot(
                along_y[:, j * cols:(j + 1) * cols], fx, preferred_element_type=F32
            )

    own_pos.wait()

    @pl.loop(1, n)
    def _(i):
        pos_copy(me, lax.rem(me + n - i, n)).wait_recv()

    for s in range(n):
        pair = pos_in[s].astype(F32)
        pos_row[0:1, s * cap:(s + 1) * cap] = ((pair[0:1] - 1.0) * 64.0 + pair[1:2])[:, 0:cap]
    for i in range(places // 128):
        place = (iota((128, slots), 0) + i * 128).astype(F32)
        placer[i * 128:(i + 1) * 128, :] = (place == pos_row[0:1, :]).astype(F32).astype(BF16)

    own_bricks.wait()

    @pl.loop(1, n)
    def _(i):
        brick_copy(me, lax.rem(me + n - i, n)).wait_recv()

    for c in range(depth):
        for d in range(height):
            at = (c * height + d) * cols
            if d % 2 == 0:
                added = jnp.dot(placer[...], arrived[:, at:at + 2 * cols], preferred_element_type=F32)
            joined[:, c, d, :, :] = added[:, (d % 2) * cols:(d % 2 + 1) * cols].reshape(
                block_planes, block_rows, cols
            )

    @pl.loop(0, block_planes)
    def _(i):
        for c in range(depth):
            z = i * depth + c
            for d in range(height):
                work[pl.ds(z * rows + d * block_rows, block_rows), :] = (
                    1.0 + joined[i, c, d]
                ) / blurred[z, d * block_rows:(d + 1) * block_rows, :]

    own_rows(work, pad2)
    for c in range(CHUNKS):
        halo_start(pad2, 1, c)
    for c in range(CHUNKS):
        halo_wait(pad2, 1, c)
        z_pass(pad2, bz, c)

    def view_copy(peer, owner, c):
        return pltpu.make_async_remote_copy(
            src_ref=back.at[pl.ds(c * zpart, zpart), pl.ds(pl.multiple_of(peer * share, share), share), :],
            dst_ref=from_views.at[owner, pl.ds(c * zpart, zpart), :, :],
            send_sem=view_send.at[peer, c],
            recv_sem=view_recv.at[owner, c],
            device_id={"view": peer},
            device_id_type=pl.DeviceIdType.MESH,
        )

    for c in range(CHUNKS):
        @pl.loop(0, zpart // 2, unroll=2)
        def _(i):
            z = c * zpart + 2 * i
            along_y = y_pass(by, z)
            for j in range(2):
                back[z + j] = along_y[:, j * cols:(j + 1) * cols]

        @pl.loop(1, nv)
        def _(i):
            view_copy(lax.rem(mv + i, nv), mv, c).start()

    first = pl.multiple_of(mv * share, share)

    @pl.loop(0, planes)
    def _(z):
        out[z] = jnp.dot(
            back[z, pl.ds(first, share), :], x_tables[mv], preferred_element_type=F32
        )

    @pl.loop(1, nv)
    def _(i):
        xt_copy(mv, lax.rem(mv + i, nv)).wait_recv()

    for c in range(CHUNKS):
        @pl.loop(1, nv)
        def _(i):
            view_copy(mv, lax.rem(mv + i, nv), c).wait_recv()

        @pl.loop(0, zpart)
        def _(i):
            z = c * zpart + i
            total = out[z]
            for v in range(1, nv):
                other = lax.rem(mv + v, nv)
                total = total + jnp.dot(
                    from_views[other, z], x_tables[other], preferred_element_type=F32
                )
            out[z] = est[pl.ds(pl.multiple_of(z * rows + first, share), share), :] * total * (1.0 / nv)

    for c in range(CHUNKS):
        halo_sent(pad1, 0, c)
        halo_sent(pad2, 1, c)

        @pl.loop(1, nv)
        def _(i):
            view_copy(lax.rem(mv + i, nv), mv, c).wait_send()

    @pl.loop(1, nv)
    def _(i):
        xt_copy(lax.rem(mv + i, nv), mv).wait_send()

    @pl.loop(1, n)
    def _(i):
        peer = lax.rem(me + i, n)
        brick_copy(peer, me).wait_send()
        pos_copy(peer, me).wait_send()


def shards(
    estimate, raw_bricks, brick_slab, brick_pos, off_z, frac_z, off_y, frac_y, off_x, frac_x,
    psf_z, psf_y, psf_x,
):
    planes, rows, cols = estimate.shape
    _, bricks, depth, height, _ = raw_bricks.shape
    n, nv = lax.axis_size("gz"), lax.axis_size("view")
    taps_z, taps_l = psf_z.shape[1], psf_x.shape[1]
    cells = depth * height
    wide = cells * cols
    cap = max(2, 2 * bricks // n)
    slots = n * cap
    share = rows // nv
    block_planes, block_rows = planes // depth, rows // height
    places = block_planes * block_rows
    dims = (planes, rows, cols, depth, height, bricks, n, nv, taps_z, taps_l)
    vmem = pl.BlockSpec(memory_space=pltpu.VMEM)
    smem = pl.BlockSpec(memory_space=pltpu.SMEM)
    dma = pltpu.SemaphoreType.DMA
    return pl.pallas_call(
        functools.partial(step, dims),
        out_shape=jax.ShapeDtypeStruct((planes, share, cols), F32),
        in_specs=[vmem] * 4 + [smem] * 4 + [vmem] * 2 + [smem] * 3,
        out_specs=vmem,
        scratch_shapes=[
            pltpu.VMEM((rows, 3 * planes, cols), BF16),
            pltpu.VMEM((rows, 3 * planes, cols), BF16),
            pltpu.VMEM((rows * planes, cols), F32),
            pltpu.VMEM((planes, rows, cols), F32),
            pltpu.VMEM((block_planes, depth, height, block_rows, cols), F32),
            pltpu.VMEM((wide, wide), BF16),
            pltpu.VMEM((bricks, wide), BF16),
            pltpu.VMEM((slots, wide), BF16),
            pltpu.VMEM((slots, wide), BF16),
            pltpu.VMEM((n, 16, 128), BF16),
            pltpu.VMEM((n, 16, 128), BF16),
            pltpu.VMEM((8, slots), F32),
            pltpu.VMEM((places, slots), BF16),
            pltpu.VMEM((planes, rows, cols), BF16),
            pltpu.VMEM((nv, planes, share, cols), BF16),
            pltpu.VMEM((nv, cols, cols), BF16),
            pltpu.VMEM((1, bricks), jnp.int32),
            dma((2, 2, CHUNKS)),
            dma((2, 2, CHUNKS)),
            dma((n,)),
            dma((n,)),
            dma((n,)),
            dma((n,)),
            dma((nv, CHUNKS)),
            dma((nv, CHUNKS)),
            dma((nv,)),
            dma((nv,)),
            dma((2,)),
        ],
        compiler_params=pltpu.CompilerParams(
            collective_id=0, has_side_effects=True, vmem_limit_bytes=48 * 1024 * 1024
        ),
    )(
        estimate.reshape(planes * rows, cols),
        raw_bricks.reshape(bricks, wide),
        brick_slab.reshape(1, bricks),
        brick_pos,
        off_z, frac_z, off_y, frac_y, off_x, frac_x, psf_z, psf_y, psf_x,
    )


def solution(mesh):
    in_specs = (
        P("gz", None, None),
        P("view", "gz", None, None, None),
        P("view", "gz", None),
        P("view", "gz"),
    ) + (P("view", None),) * 9
    out_specs = P("gz", "view", None)
    return jax.shard_map(shards, mesh=mesh, in_specs=in_specs, out_specs=out_specs, check_vma=False)
```

```python
import functools

import jax
import jax.numpy as jnp
from jax import lax
from jax.experimental import pallas as pl
from jax.experimental.pallas import tpu as pltpu
from jax.sharding import PartitionSpec as P

BF16 = jnp.bfloat16
F32 = jnp.float32
CHUNKS = 4


def iota(shape, dim):
    return lax.broadcasted_iota(jnp.int32, shape, dim)


def tap_table(psf, count, which):
    normed = psf[...] / jnp.sum(psf[...], axis=1, keepdims=True)
    table = jnp.zeros(which.shape, F32)
    for k in range(count):
        table = jnp.where(which == k, jnp.broadcast_to(normed[0:1, k:k + 1], which.shape), table)
    return table.astype(BF16)


def small_weight(off, frac, column, source):
    fraction = jnp.broadcast_to(frac[0:1, column:column + 1], (1, 128))
    offset = jnp.broadcast_to(off[0:1, column:column + 1], (1, 128))
    low = (1.0 - fraction).astype(BF16).astype(F32)
    high = fraction.astype(BF16).astype(F32)
    return jnp.where(offset == source, low, 0.0) + jnp.where(offset + 1 == source, high, 0.0)


def step(
    dims,
    est, raw, slab, pos, off_z, frac_z, off_y, frac_y, off_x, frac_x, psf_z, psf_y, psf_x,
    out,
    pad1, pad2, work, blurred, joined, weights, by_cell, mixed, outgoing, arrived, pos_out, pos_in, pos_row,
    placer, back, from_views, x_tables, slot_scr,
    halo_send, halo_recv, share_send, share_recv, pass_send, pass_recv, brick_send, brick_recv, pos_send, pos_recv, view_send, view_recv,
    xt_send, xt_recv, own_sem,
):
    planes, rows, cols, depth, height, bricks, n, nv, taps_z, taps_l = dims
    cells = depth * height
    wide = cells * cols
    cap = max(2, 2 * bricks // n)
    slots = n * cap
    block_planes = planes // depth
    block_rows = rows // height
    places = block_planes * block_rows
    half = taps_z // 2
    lat = taps_l // 2
    share = rows // nv
    part = rows // CHUNKS
    zpart = planes // CHUNKS
    piece = share // 2
    me = lax.axis_index("gz")
    mv = lax.axis_index("view")

    barrier = pltpu.get_barrier_semaphore()

    @pl.loop(1, n)
    def _(i):
        pl.semaphore_signal(barrier, inc=1, device_id={"gz": lax.rem(me + i, n)})

    @pl.loop(1, nv)
    def _(i):
        pl.semaphore_signal(barrier, inc=1, device_id={"view": lax.rem(mv + i, nv)})

    def own_rows(source, pad, start, count):
        @pl.loop(0, count, unroll=8)
        def _(i):
            y = start + i
            pad[y, pl.ds(planes, planes), :] = source[pl.ds(y, planes, stride=rows), :].astype(BF16)

    own_rows(est, pad1, 0, rows)

    pl.semaphore_wait(barrier, n - 1 + nv - 1)

    left, right = lax.rem(me + n - 1, n), lax.rem(me + 1, n)

    def neighbours(start_row, count, pad, send_sems, recv_sems, c):
        def copy(side):
            return pltpu.make_async_remote_copy(
                src_ref=pad.at[pl.ds(start_row, count), pl.ds(planes, planes), :],
                dst_ref=pad.at[pl.ds(start_row, count), pl.ds(side * 2 * planes, planes), :],
                send_sem=send_sems.at[side, c],
                recv_sem=recv_sems.at[side, c],
                device_id={"gz": (right, left)[side]},
                device_id_type=pl.DeviceIdType.MESH,
            )

        return copy

    def on_sides(to_right, to_left, arriving=False):
        @pl.when(me > 0 if arriving else me < n - 1)
        def _():
            to_right()

        @pl.when(me < n - 1 if arriving else me > 0)
        def _():
            to_left()

    def share_copy(c):
        return neighbours(mv * share + c * piece, piece, pad1, share_send, share_recv, c)

    def pass_copy(side, c, peer, owner):
        block = pad1.at[pl.ds(owner * share + c * piece, piece), pl.ds(side * 2 * planes, planes), :]
        return pltpu.make_async_remote_copy(
            src_ref=block,
            dst_ref=block,
            send_sem=pass_send.at[peer, side, c],
            recv_sem=pass_recv.at[owner, side, c],
            device_id={"view": peer},
            device_id_type=pl.DeviceIdType.MESH,
        )

    def halo(c):
        return neighbours(c * part, part, pad2, halo_send, halo_recv, c)

    for c in range(2):
        copy = share_copy(c)
        on_sides(copy(0).start, copy(1).start)

    @pl.when(me == 0)
    def _():
        for pad in (pad1, pad2):
            pad[:, pl.ds(0, planes), :] = jnp.zeros((rows, planes, cols), BF16)

    @pl.when(me == n - 1)
    def _():
        for pad in (pad1, pad2):
            pad[:, pl.ds(2 * planes, planes), :] = jnp.zeros((rows, planes, cols), BF16)

    source = iota((cols, cols), 0)
    low = (1.0 - frac_x[...]).astype(BF16).astype(F32)
    high = frac_x[...].astype(BF16).astype(F32)
    along = jnp.where(source == off_x[...], low, 0.0) + jnp.where(source == off_x[...] + 1, high, 0.0)
    along_b = along.astype(BF16)
    quarter = bricks * cells // 4
    for i in range(4):
        work[i * quarter:(i + 1) * quarter, :] = jnp.dot(
            raw[i * quarter:(i + 1) * quarter, :], along_b, preferred_element_type=F32
        ).astype(BF16).astype(F32)
    for q in range(cells):
        by_cell[:, q * cols:(q + 1) * cols] = work[pl.ds(q, bricks, stride=cells), :].astype(BF16)
    unit = (iota((cols, cols), 0) == iota((cols, cols), 1)).astype(F32)
    for a in range(depth):
        for c in range(depth):
            wz = small_weight(off_z, frac_z, c, a)
            for e in range(height):
                for d in range(height):
                    wy = small_weight(off_y, frac_y, d, e)
                    weights[
                        (a * height + e) * cols:(a * height + e + 1) * cols,
                        (c * height + d) * cols:(c * height + d + 1) * cols,
                    ] = (unit * (wz * wy)).astype(BF16)
    for i in range(wide // 256):
        mixed[:, i * 256:(i + 1) * 256] = jnp.dot(
            by_cell[...], weights[:, i * 256:(i + 1) * 256], preferred_element_type=F32
        ).astype(BF16)

    slab_v = slab[...]
    member = iota((n, bricks), 0) == slab_v
    before = (iota((bricks, bricks), 0) < iota((bricks, bricks), 1)).astype(F32).astype(BF16)
    earlier = jnp.dot(member.astype(F32).astype(BF16), before, preferred_element_type=F32)
    order = jnp.sum(jnp.where(member, earlier, 0.0), axis=0, keepdims=True).astype(jnp.int32)
    slot_scr[...] = slab_v * cap + order
    pos_v = pos[...]
    row16 = iota((16, bricks), 0)
    pos_pair = jnp.where(
        row16 == 0, pos_v // 64 + 1, jnp.where(row16 == 1, lax.rem(pos_v, 64), 0)
    ).astype(F32).astype(BF16)
    for i in range(slots // 256):
        chosen = ((iota((256, bricks), 0) + i * 256) == slot_scr[...]).astype(F32).astype(BF16)
        outgoing[i * 256:(i + 1) * 256, :] = jnp.dot(
            chosen, mixed[...], preferred_element_type=F32
        ).astype(BF16)
        slot_pos = lax.dot_general(
            pos_pair, chosen, (((1,), (1,)), ((), ())), preferred_element_type=F32
        )
        for j in range(256 // cap):
            pos_out[i * (256 // cap) + j, :, 0:cap] = slot_pos[:, j * cap:(j + 1) * cap].astype(BF16)

    def brick_copy(peer, owner):
        return pltpu.make_async_remote_copy(
            src_ref=outgoing.at[pl.ds(pl.multiple_of(peer * cap, cap), cap), :],
            dst_ref=arrived.at[pl.ds(pl.multiple_of(owner * cap, cap), cap), :],
            send_sem=brick_send.at[peer],
            recv_sem=brick_recv.at[owner],
            device_id={"gz": peer},
            device_id_type=pl.DeviceIdType.MESH,
        )

    def pos_copy(peer, owner):
        return pltpu.make_async_remote_copy(
            src_ref=pos_out.at[peer],
            dst_ref=pos_in.at[owner],
            send_sem=pos_send.at[peer],
            recv_sem=pos_recv.at[owner],
            device_id={"gz": peer},
            device_id_type=pl.DeviceIdType.MESH,
        )

    @pl.loop(1, n)
    def _(i):
        peer = lax.rem(me + i, n)
        brick_copy(peer, me).start()
        pos_copy(peer, me).start()

    mine = pl.ds(pl.multiple_of(me * cap, cap), cap)
    own_bricks = pltpu.make_async_copy(outgoing.at[mine, :], arrived.at[mine, :], own_sem.at[0])
    own_pos = pltpu.make_async_copy(pos_out.at[me], pos_in.at[me], own_sem.at[1])
    own_bricks.start()
    own_pos.start()

    def true_row(r):
        return lax.rem(r, block_rows) * height + r // block_rows

    ii, jj = iota((rows, rows), 0), iota((rows, rows), 1)
    fy = tap_table(psf_y, taps_l, jj - true_row(ii) + lat)
    by = tap_table(psf_y, taps_l, ii - true_row(jj) + lat)
    ci, cj = iota((cols, cols), 0), iota((cols, cols), 1)
    fx = tap_table(psf_x, taps_l, ci - cj + lat)
    x_tables[mv] = tap_table(psf_x, taps_l, cj - ci + lat)
    zi, zj = iota((planes, 3 * planes), 0), iota((planes, 3 * planes), 1)
    fz = tap_table(psf_z, taps_z, zj - zi - (planes - half))
    bz = tap_table(psf_z, taps_z, planes + half + zi - zj)

    def xt_copy(peer, owner):
        return pltpu.make_async_remote_copy(
            src_ref=x_tables.at[mv],
            dst_ref=x_tables.at[owner],
            send_sem=xt_send.at[peer],
            recv_sem=xt_recv.at[owner],
            device_id={"view": peer},
            device_id_type=pl.DeviceIdType.MESH,
        )

    @pl.loop(1, nv)
    def _(i):
        xt_copy(lax.rem(mv + i, nv), mv).start()

    def z_pass(pad, table, start, count):
        @pl.loop(0, count // 4, unroll=4)
        def _(i):
            y = start + i * 4
            block = jnp.concatenate([pad[y + j] for j in range(4)], axis=1)
            result = jnp.dot(table, block, preferred_element_type=F32)
            result = result.astype(BF16).astype(F32)
            for j in range(4):
                work[pl.ds((y + j) * planes, planes), :] = result[:, j * cols:(j + 1) * cols]

    def y_pass(table, z):
        block = jnp.concatenate(
            [work[pl.ds(z + j, rows, stride=planes), :].astype(BF16) for j in range(2)], axis=1
        )
        return jnp.dot(table, block, preferred_element_type=F32).astype(BF16)

    def pass_on(side, c):
        @pl.loop(1, nv)
        def _(i):
            pass_copy(side, c, lax.rem(mv + i, nv), mv).start()

    def pass_take(side, c, owner):
        pass_copy(side, c, mv, owner).wait_recv()

    def pass_sent(side, c):
        @pl.loop(1, nv)
        def _(i):
            pass_copy(side, c, lax.rem(mv + i, nv), mv).wait_send()

    for c in range(2):
        copy = share_copy(c)
        on_sides(copy(0).wait_recv, copy(1).wait_recv, arriving=True)
        on_sides(lambda: pass_on(0, c), lambda: pass_on(1, c), arriving=True)
    z_pass(pad1, fz, mv * share, share)
    for v in range(1, nv):
        owner = lax.rem(mv + nv - v, nv)
        for c in range(2):
            on_sides(lambda: pass_take(0, c, owner), lambda: pass_take(1, c, owner), arriving=True)
            z_pass(pad1, fz, owner * share + c * piece, piece)

    @pl.loop(0, planes // 2, unroll=4)
    def _(i):
        along_y = y_pass(fy, 2 * i)
        for j in range(2):
            blurred[2 * i + j] = jnp.dot(
                along_y[:, j * cols:(j + 1) * cols], fx, preferred_element_type=F32
            )

    own_pos.wait()

    @pl.loop(1, n)
    def _(i):
        pos_copy(me, lax.rem(me + n - i, n)).wait_recv()

    for s in range(n):
        pair = pos_in[s].astype(F32)
        pos_row[0:1, s * cap:(s + 1) * cap] = ((pair[0:1] - 1.0) * 64.0 + pair[1:2])[:, 0:cap]
    for i in range(places // 128):
        place = (iota((128, slots), 0) + i * 128).astype(F32)
        placer[i * 128:(i + 1) * 128, :] = (place == pos_row[0:1, :]).astype(F32).astype(BF16)

    own_bricks.wait()

    @pl.loop(1, n)
    def _(i):
        brick_copy(me, lax.rem(me + n - i, n)).wait_recv()

    for c in range(depth):
        for d in range(height):
            at = (c * height + d) * cols
            if d % 2 == 0:
                added = jnp.dot(placer[...], arrived[:, at:at + 2 * cols], preferred_element_type=F32)
            joined[:, c, d, :, :] = added[:, (d % 2) * cols:(d % 2 + 1) * cols].reshape(
                block_planes, block_rows, cols
            )

    for c in range(CHUNKS):
        d, at_row = c * part // block_rows, c * part % block_rows

        @pl.loop(0, block_planes)
        def _(i):
            for k in range(depth):
                z = i * depth + k
                work[pl.ds(z * rows + c * part, part), :] = (
                    1.0 + joined[i, k, d, at_row:at_row + part, :]
                ) / blurred[z, c * part:(c + 1) * part, :]

        own_rows(work, pad2, c * part, part)
        copy = halo(c)
        on_sides(copy(0).start, copy(1).start)
    for c in range(CHUNKS):
        copy = halo(c)
        on_sides(copy(0).wait_recv, copy(1).wait_recv, arriving=True)
        z_pass(pad2, bz, c * part, part)

    def view_copy(peer, owner, c):
        return pltpu.make_async_remote_copy(
            src_ref=back.at[pl.ds(c * zpart, zpart), pl.ds(pl.multiple_of(peer * share, share), share), :],
            dst_ref=from_views.at[owner, pl.ds(c * zpart, zpart), :, :],
            send_sem=view_send.at[peer, c],
            recv_sem=view_recv.at[owner, c],
            device_id={"view": peer},
            device_id_type=pl.DeviceIdType.MESH,
        )

    for c in range(CHUNKS):
        @pl.loop(0, zpart // 2, unroll=4)
        def _(i):
            z = c * zpart + 2 * i
            along_y = y_pass(by, z)
            for j in range(2):
                back[z + j] = along_y[:, j * cols:(j + 1) * cols]

        @pl.loop(1, nv)
        def _(i):
            view_copy(lax.rem(mv + i, nv), mv, c).start()

    first = pl.multiple_of(mv * share, share)

    @pl.loop(1, nv)
    def _(i):
        xt_copy(mv, lax.rem(mv + i, nv)).wait_recv()

    for c in range(CHUNKS):
        @pl.loop(1, nv)
        def _(i):
            view_copy(mv, lax.rem(mv + i, nv), c).wait_recv()

        planes_c = slice(c * zpart, (c + 1) * zpart)
        total = jnp.dot(
            back[planes_c, pl.ds(first, share), :].reshape(zpart * share, cols),
            x_tables[mv],
            preferred_element_type=F32,
        )
        for v in range(1, nv):
            other = lax.rem(mv + v, nv)
            total = total + jnp.dot(
                from_views[other, planes_c].reshape(zpart * share, cols),
                x_tables[other],
                preferred_element_type=F32,
            )
        for k in range(zpart):
            z = c * zpart + k
            out[z] = (
                est[pl.ds(pl.multiple_of(z * rows + first, share), share), :]
                * total[k * share:(k + 1) * share]
                * (1.0 / nv)
            )

    for c in range(2):
        copy = share_copy(c)
        on_sides(copy(0).wait_send, copy(1).wait_send)
        on_sides(lambda: pass_sent(0, c), lambda: pass_sent(1, c), arriving=True)
    for c in range(CHUNKS):
        copy = halo(c)
        on_sides(copy(0).wait_send, copy(1).wait_send)

        @pl.loop(1, nv)
        def _(i):
            view_copy(lax.rem(mv + i, nv), mv, c).wait_send()

    @pl.loop(1, nv)
    def _(i):
        xt_copy(lax.rem(mv + i, nv), mv).wait_send()

    @pl.loop(1, n)
    def _(i):
        peer = lax.rem(me + i, n)
        brick_copy(peer, me).wait_send()
        pos_copy(peer, me).wait_send()


def shards(
    estimate, raw_bricks, brick_slab, brick_pos, off_z, frac_z, off_y, frac_y, off_x, frac_x,
    psf_z, psf_y, psf_x,
):
    planes, rows, cols = estimate.shape
    _, bricks, depth, height, _ = raw_bricks.shape
    n, nv = lax.axis_size("gz"), lax.axis_size("view")
    taps_z, taps_l = psf_z.shape[1], psf_x.shape[1]
    cells = depth * height
    wide = cells * cols
    cap = max(2, 2 * bricks // n)
    slots = n * cap
    share = rows // nv
    block_planes, block_rows = planes // depth, rows // height
    places = block_planes * block_rows
    dims = (planes, rows, cols, depth, height, bricks, n, nv, taps_z, taps_l)
    vmem = pl.BlockSpec(memory_space=pltpu.VMEM)
    dma = pltpu.SemaphoreType.DMA
    return pl.pallas_call(
        functools.partial(step, dims),
        out_shape=jax.ShapeDtypeStruct((planes, share, cols), F32),
        in_specs=[vmem] * 13,
        out_specs=vmem,
        scratch_shapes=[
            pltpu.VMEM((rows, 3 * planes, cols), BF16),
            pltpu.VMEM((rows, 3 * planes, cols), BF16),
            pltpu.VMEM((max(rows * planes, bricks * cells), cols), F32),
            pltpu.VMEM((planes, rows, cols), F32),
            pltpu.VMEM((block_planes, depth, height, block_rows, cols), F32),
            pltpu.VMEM((wide, wide), BF16),
            pltpu.VMEM((bricks, wide), BF16),
            pltpu.VMEM((bricks, wide), BF16),
            pltpu.VMEM((slots, wide), BF16),
            pltpu.VMEM((slots, wide), BF16),
            pltpu.VMEM((n, 16, 128), BF16),
            pltpu.VMEM((n, 16, 128), BF16),
            pltpu.VMEM((8, slots), F32),
            pltpu.VMEM((places, slots), BF16),
            pltpu.VMEM((planes, rows, cols), BF16),
            pltpu.VMEM((nv, planes, share, cols), BF16),
            pltpu.VMEM((nv, cols, cols), BF16),
            pltpu.VMEM((1, bricks), jnp.int32),
            dma((2, CHUNKS)),
            dma((2, CHUNKS)),
            dma((2, 2)),
            dma((2, 2)),
            dma((nv, 2, 2)),
            dma((nv, 2, 2)),
            dma((n,)),
            dma((n,)),
            dma((n,)),
            dma((n,)),
            dma((nv, CHUNKS)),
            dma((nv, CHUNKS)),
            dma((nv,)),
            dma((nv,)),
            dma((2,)),
        ],
        compiler_params=pltpu.CompilerParams(
            collective_id=0, has_side_effects=True, vmem_limit_bytes=48 * 1024 * 1024
        ),
    )(
        estimate.reshape(planes * rows, cols),
        raw_bricks.reshape(bricks * cells, cols),
        brick_slab.reshape(1, bricks),
        brick_pos,
        off_z, frac_z, off_y, frac_y, off_x, frac_x, psf_z, psf_y, psf_x,
    )


def solution(mesh):
    in_specs = (
        P("gz", None, None),
        P("view", "gz", None, None, None),
        P("view", "gz", None),
        P("view", "gz"),
    ) + (P("view", None),) * 9
    out_specs = P("gz", "view", None)
    return jax.shard_map(shards, mesh=mesh, in_specs=in_specs, out_specs=out_specs, check_vma=False)
```

```python
import functools

import jax
import jax.numpy as jnp
from jax import lax
from jax.experimental import pallas as pl
from jax.experimental.pallas import tpu as pltpu
from jax.sharding import PartitionSpec as P

BF16 = jnp.bfloat16
F32 = jnp.float32
CHUNKS = 4


def iota(shape, dim):
    return lax.broadcasted_iota(jnp.int32, shape, dim)


def tap_table(psf, count, which):
    normed = psf[...] / jnp.sum(psf[...], axis=1, keepdims=True)
    table = jnp.zeros(which.shape, F32)
    for k in range(count):
        table = jnp.where(which == k, jnp.broadcast_to(normed[0:1, k:k + 1], which.shape), table)
    return table.astype(BF16)


def small_weight(off, frac, column, source):
    fraction = jnp.broadcast_to(frac[0:1, column:column + 1], (1, 128))
    offset = jnp.broadcast_to(off[0:1, column:column + 1], (1, 128))
    low = (1.0 - fraction).astype(BF16).astype(F32)
    high = fraction.astype(BF16).astype(F32)
    return jnp.where(offset == source, low, 0.0) + jnp.where(offset + 1 == source, high, 0.0)


def step(
    dims,
    *refs,
):
    operands, out, fetched, fetch_sem = refs[:13], refs[13], refs[14:27], refs[27]
    est, raw, slab, pos, off_z, frac_z, off_y, frac_y, off_x, frac_x, psf_z, psf_y, psf_x = fetched
    body(
        dims, operands, fetched, fetch_sem,
        est, raw, slab, pos, off_z, frac_z, off_y, frac_y, off_x, frac_x, psf_z, psf_y, psf_x,
        out, *refs[28:],
    )


def body(
    dims, operands, fetched, fetch_sem,
    est, raw, slab, pos, off_z, frac_z, off_y, frac_y, off_x, frac_x, psf_z, psf_y, psf_x,
    out,
    pad1, pad2, work, blurred, joined, weights, by_cell, mixed, outgoing, arrived, pos_out, pos_in, pos_row,
    placer, back, from_views, x_tables, slot_scr,
    halo_send, halo_recv, share_send, share_recv, pass_send, pass_recv, brick_send, brick_recv, pos_send, pos_recv, view_send, view_recv,
    xt_send, xt_recv, own_sem,
):
    planes, rows, cols, depth, height, bricks, n, nv, taps_z, taps_l = dims
    cells = depth * height
    wide = cells * cols
    cap = max(2, 2 * bricks // n)
    slots = n * cap
    block_planes = planes // depth
    block_rows = rows // height
    places = block_planes * block_rows
    half = taps_z // 2
    lat = taps_l // 2
    share = rows // nv
    part = rows // CHUNKS
    zpart = planes // CHUNKS
    piece = share // 2
    me = lax.axis_index("gz")
    mv = lax.axis_index("view")

    fetches = [
        pltpu.make_async_copy(operands[i], fetched[i], fetch_sem.at[i]) for i in range(len(operands))
    ]
    for fetch in fetches:
        fetch.start()

    barrier = pltpu.get_barrier_semaphore()

    @pl.loop(1, n)
    def _(i):
        pl.semaphore_signal(barrier, inc=1, device_id={"gz": lax.rem(me + i, n)})

    @pl.loop(1, nv)
    def _(i):
        pl.semaphore_signal(barrier, inc=1, device_id={"view": lax.rem(mv + i, nv)})

    def own_rows(source, pad, start, count):
        @pl.loop(0, count, unroll=8)
        def _(i):
            y = start + i
            pad[y, pl.ds(planes, planes), :] = source[pl.ds(y, planes, stride=rows), :].astype(BF16)

    fetches[0].wait()
    own_rows(est, pad1, 0, rows)

    pl.semaphore_wait(barrier, n - 1 + nv - 1)

    left, right = lax.rem(me + n - 1, n), lax.rem(me + 1, n)

    def neighbours(start_row, count, pad, send_sems, recv_sems, c):
        def copy(side):
            return pltpu.make_async_remote_copy(
                src_ref=pad.at[pl.ds(start_row, count), pl.ds(planes, planes), :],
                dst_ref=pad.at[pl.ds(start_row, count), pl.ds(side * 2 * planes, planes), :],
                send_sem=send_sems.at[side, c],
                recv_sem=recv_sems.at[side, c],
                device_id={"gz": (right, left)[side]},
                device_id_type=pl.DeviceIdType.MESH,
            )

        return copy

    def on_sides(to_right, to_left, arriving=False):
        @pl.when(me > 0 if arriving else me < n - 1)
        def _():
            to_right()

        @pl.when(me < n - 1 if arriving else me > 0)
        def _():
            to_left()

    def share_copy(c):
        return neighbours(mv * share + c * piece, piece, pad1, share_send, share_recv, c)

    def pass_copy(side, c, peer, owner):
        block = pad1.at[pl.ds(owner * share + c * piece, piece), pl.ds(side * 2 * planes, planes), :]
        return pltpu.make_async_remote_copy(
            src_ref=block,
            dst_ref=block,
            send_sem=pass_send.at[peer, side, c],
            recv_sem=pass_recv.at[owner, side, c],
            device_id={"view": peer},
            device_id_type=pl.DeviceIdType.MESH,
        )

    def halo(c):
        return neighbours(c * part, part, pad2, halo_send, halo_recv, c)

    for c in range(2):
        copy = share_copy(c)
        on_sides(copy(0).start, copy(1).start)

    @pl.when(me == 0)
    def _():
        for pad in (pad1, pad2):
            pad[:, pl.ds(0, planes), :] = jnp.zeros((rows, planes, cols), BF16)

    @pl.when(me == n - 1)
    def _():
        for pad in (pad1, pad2):
            pad[:, pl.ds(2 * planes, planes), :] = jnp.zeros((rows, planes, cols), BF16)

    for fetch in fetches[1:]:
        fetch.wait()
    source = iota((cols, cols), 0)
    low = (1.0 - frac_x[...]).astype(BF16).astype(F32)
    high = frac_x[...].astype(BF16).astype(F32)
    along = jnp.where(source == off_x[...], low, 0.0) + jnp.where(source == off_x[...] + 1, high, 0.0)
    along_b = along.astype(BF16)
    quarter = bricks * cells // 4
    for i in range(4):
        work[i * quarter:(i + 1) * quarter, :] = jnp.dot(
            raw[i * quarter:(i + 1) * quarter, :], along_b, preferred_element_type=F32
        ).astype(BF16).astype(F32)
    for q in range(cells):
        by_cell[:, q * cols:(q + 1) * cols] = work[pl.ds(q, bricks, stride=cells), :].astype(BF16)
    unit = (iota((cols, cols), 0) == iota((cols, cols), 1)).astype(F32)
    for a in range(depth):
        for c in range(depth):
            wz = small_weight(off_z, frac_z, c, a)
            for e in range(height):
                for d in range(height):
                    wy = small_weight(off_y, frac_y, d, e)
                    weights[
                        (a * height + e) * cols:(a * height + e + 1) * cols,
                        (c * height + d) * cols:(c * height + d + 1) * cols,
                    ] = (unit * (wz * wy)).astype(BF16)
    for i in range(wide // 256):
        mixed[:, i * 256:(i + 1) * 256] = jnp.dot(
            by_cell[...], weights[:, i * 256:(i + 1) * 256], preferred_element_type=F32
        ).astype(BF16)

    slab_v = slab[...]
    member = iota((n, bricks), 0) == slab_v
    before = (iota((bricks, bricks), 0) < iota((bricks, bricks), 1)).astype(F32).astype(BF16)
    earlier = jnp.dot(member.astype(F32).astype(BF16), before, preferred_element_type=F32)
    order = jnp.sum(jnp.where(member, earlier, 0.0), axis=0, keepdims=True).astype(jnp.int32)
    slot_scr[...] = slab_v * cap + order
    pos_v = pos[...]
    row16 = iota((16, bricks), 0)
    pos_pair = jnp.where(
        row16 == 0, pos_v // 64 + 1, jnp.where(row16 == 1, lax.rem(pos_v, 64), 0)
    ).astype(F32).astype(BF16)
    for i in range(slots // 256):
        chosen = ((iota((256, bricks), 0) + i * 256) == slot_scr[...]).astype(F32).astype(BF16)
        outgoing[i * 256:(i + 1) * 256, :] = jnp.dot(
            chosen, mixed[...], preferred_element_type=F32
        ).astype(BF16)
        slot_pos = lax.dot_general(
            pos_pair, chosen, (((1,), (1,)), ((), ())), preferred_element_type=F32
        )
        for j in range(256 // cap):
            pos_out[i * (256 // cap) + j, :, 0:cap] = slot_pos[:, j * cap:(j + 1) * cap].astype(BF16)

    def brick_copy(peer, owner):
        return pltpu.make_async_remote_copy(
            src_ref=outgoing.at[pl.ds(pl.multiple_of(peer * cap, cap), cap), :],
            dst_ref=arrived.at[pl.ds(pl.multiple_of(owner * cap, cap), cap), :],
            send_sem=brick_send.at[peer],
            recv_sem=brick_recv.at[owner],
            device_id={"gz": peer},
            device_id_type=pl.DeviceIdType.MESH,
        )

    def pos_copy(peer, owner):
        return pltpu.make_async_remote_copy(
            src_ref=pos_out.at[peer],
            dst_ref=pos_in.at[owner],
            send_sem=pos_send.at[peer],
            recv_sem=pos_recv.at[owner],
            device_id={"gz": peer},
            device_id_type=pl.DeviceIdType.MESH,
        )

    @pl.loop(1, n)
    def _(i):
        peer = lax.rem(me + i, n)
        brick_copy(peer, me).start()
        pos_copy(peer, me).start()

    mine = pl.ds(pl.multiple_of(me * cap, cap), cap)
    own_bricks = pltpu.make_async_copy(outgoing.at[mine, :], arrived.at[mine, :], own_sem.at[0])
    own_pos = pltpu.make_async_copy(pos_out.at[me], pos_in.at[me], own_sem.at[1])
    own_bricks.start()
    own_pos.start()

    def true_row(r):
        return lax.rem(r, block_rows) * height + r // block_rows

    ii, jj = iota((rows, rows), 0), iota((rows, rows), 1)
    fy = tap_table(psf_y, taps_l, jj - true_row(ii) + lat)
    by = tap_table(psf_y, taps_l, ii - true_row(jj) + lat)
    ci, cj = iota((cols, cols), 0), iota((cols, cols), 1)
    fx = tap_table(psf_x, taps_l, ci - cj + lat)
    x_tables[mv] = tap_table(psf_x, taps_l, cj - ci + lat)
    zi, zj = iota((planes, 3 * planes), 0), iota((planes, 3 * planes), 1)
    fz = tap_table(psf_z, taps_z, zj - zi - (planes - half))
    bz = tap_table(psf_z, taps_z, planes + half + zi - zj)

    def xt_copy(peer, owner):
        return pltpu.make_async_remote_copy(
            src_ref=x_tables.at[mv],
            dst_ref=x_tables.at[owner],
            send_sem=xt_send.at[peer],
            recv_sem=xt_recv.at[owner],
            device_id={"view": peer},
            device_id_type=pl.DeviceIdType.MESH,
        )

    @pl.loop(1, nv)
    def _(i):
        xt_copy(lax.rem(mv + i, nv), mv).start()

    def z_pass(pad, table, start, count):
        @pl.loop(0, count // 4, unroll=4)
        def _(i):
            y = start + i * 4
            block = jnp.concatenate([pad[y + j] for j in range(4)], axis=1)
            result = jnp.dot(table, block, preferred_element_type=F32)
            result = result.astype(BF16).astype(F32)
            for j in range(4):
                work[pl.ds((y + j) * planes, planes), :] = result[:, j * cols:(j + 1) * cols]

    def y_pass(table, z):
        block = jnp.concatenate(
            [work[pl.ds(z + j, rows, stride=planes), :].astype(BF16) for j in range(2)], axis=1
        )
        return jnp.dot(table, block, preferred_element_type=F32).astype(BF16)

    def pass_on(side, c):
        @pl.loop(1, nv)
        def _(i):
            pass_copy(side, c, lax.rem(mv + i, nv), mv).start()

    def pass_take(side, c, owner):
        pass_copy(side, c, mv, owner).wait_recv()

    def pass_sent(side, c):
        @pl.loop(1, nv)
        def _(i):
            pass_copy(side, c, lax.rem(mv + i, nv), mv).wait_send()

    for c in range(2):
        copy = share_copy(c)
        on_sides(copy(0).wait_recv, copy(1).wait_recv, arriving=True)
        on_sides(lambda: pass_on(0, c), lambda: pass_on(1, c), arriving=True)
    z_pass(pad1, fz, mv * share, share)
    for v in range(1, nv):
        owner = lax.rem(mv + nv - v, nv)
        for c in range(2):
            on_sides(lambda: pass_take(0, c, owner), lambda: pass_take(1, c, owner), arriving=True)
            z_pass(pad1, fz, owner * share + c * piece, piece)

    @pl.loop(0, planes // 2, unroll=4)
    def _(i):
        along_y = y_pass(fy, 2 * i)
        for j in range(2):
            blurred[2 * i + j] = jnp.dot(
                along_y[:, j * cols:(j + 1) * cols], fx, preferred_element_type=F32
            )

    own_pos.wait()

    @pl.loop(1, n)
    def _(i):
        pos_copy(me, lax.rem(me + n - i, n)).wait_recv()

    for s in range(n):
        pair = pos_in[s].astype(F32)
        pos_row[0:1, s * cap:(s + 1) * cap] = ((pair[0:1] - 1.0) * 64.0 + pair[1:2])[:, 0:cap]
    for i in range(places // 128):
        place = (iota((128, slots), 0) + i * 128).astype(F32)
        placer[i * 128:(i + 1) * 128, :] = (place == pos_row[0:1, :]).astype(F32).astype(BF16)

    own_bricks.wait()

    @pl.loop(1, n)
    def _(i):
        brick_copy(me, lax.rem(me + n - i, n)).wait_recv()

    for c in range(depth):
        for d in range(height):
            at = (c * height + d) * cols
            if d % 2 == 0:
                added = jnp.dot(placer[...], arrived[:, at:at + 2 * cols], preferred_element_type=F32)
            joined[:, c, d, :, :] = added[:, (d % 2) * cols:(d % 2 + 1) * cols].reshape(
                block_planes, block_rows, cols
            )

    for c in range(CHUNKS):
        d, at_row = c * part // block_rows, c * part % block_rows

        @pl.loop(0, block_planes)
        def _(i):
            for k in range(depth):
                z = i * depth + k
                work[pl.ds(z * rows + c * part, part), :] = (
                    1.0 + joined[i, k, d, at_row:at_row + part, :]
                ) / blurred[z, c * part:(c + 1) * part, :]

        own_rows(work, pad2, c * part, part)
        copy = halo(c)
        on_sides(copy(0).start, copy(1).start)
    for c in range(CHUNKS):
        copy = halo(c)
        on_sides(copy(0).wait_recv, copy(1).wait_recv, arriving=True)
        z_pass(pad2, bz, c * part, part)

    def view_copy(peer, owner, c):
        return pltpu.make_async_remote_copy(
            src_ref=back.at[pl.ds(c * zpart, zpart), pl.ds(pl.multiple_of(peer * share, share), share), :],
            dst_ref=from_views.at[owner, pl.ds(c * zpart, zpart), :, :],
            send_sem=view_send.at[peer, c],
            recv_sem=view_recv.at[owner, c],
            device_id={"view": peer},
            device_id_type=pl.DeviceIdType.MESH,
        )

    for c in range(CHUNKS):
        @pl.loop(0, zpart // 2, unroll=4)
        def _(i):
            z = c * zpart + 2 * i
            along_y = y_pass(by, z)
            for j in range(2):
                back[z + j] = along_y[:, j * cols:(j + 1) * cols]

        @pl.loop(1, nv)
        def _(i):
            view_copy(lax.rem(mv + i, nv), mv, c).start()

    first = pl.multiple_of(mv * share, share)

    @pl.loop(1, nv)
    def _(i):
        xt_copy(mv, lax.rem(mv + i, nv)).wait_recv()

    for c in range(CHUNKS):
        @pl.loop(1, nv)
        def _(i):
            view_copy(mv, lax.rem(mv + i, nv), c).wait_recv()

        planes_c = slice(c * zpart, (c + 1) * zpart)
        total = jnp.dot(
            back[planes_c, pl.ds(first, share), :].reshape(zpart * share, cols),
            x_tables[mv],
            preferred_element_type=F32,
        )
        for v in range(1, nv):
            other = lax.rem(mv + v, nv)
            total = total + jnp.dot(
                from_views[other, planes_c].reshape(zpart * share, cols),
                x_tables[other],
                preferred_element_type=F32,
            )
        for k in range(zpart):
            z = c * zpart + k
            out[z] = (
                est[pl.ds(pl.multiple_of(z * rows + first, share), share), :]
                * total[k * share:(k + 1) * share]
                * (1.0 / nv)
            )

    for c in range(2):
        copy = share_copy(c)
        on_sides(copy(0).wait_send, copy(1).wait_send)
        on_sides(lambda: pass_sent(0, c), lambda: pass_sent(1, c), arriving=True)
    for c in range(CHUNKS):
        copy = halo(c)
        on_sides(copy(0).wait_send, copy(1).wait_send)

        @pl.loop(1, nv)
        def _(i):
            view_copy(lax.rem(mv + i, nv), mv, c).wait_send()

    @pl.loop(1, nv)
    def _(i):
        xt_copy(lax.rem(mv + i, nv), mv).wait_send()

    @pl.loop(1, n)
    def _(i):
        peer = lax.rem(me + i, n)
        brick_copy(peer, me).wait_send()
        pos_copy(peer, me).wait_send()


def shards(
    estimate, raw_bricks, brick_slab, brick_pos, off_z, frac_z, off_y, frac_y, off_x, frac_x,
    psf_z, psf_y, psf_x,
):
    planes, rows, cols = estimate.shape
    _, bricks, depth, height, _ = raw_bricks.shape
    n, nv = lax.axis_size("gz"), lax.axis_size("view")
    taps_z, taps_l = psf_z.shape[1], psf_x.shape[1]
    cells = depth * height
    wide = cells * cols
    cap = max(2, 2 * bricks // n)
    slots = n * cap
    share = rows // nv
    block_planes, block_rows = planes // depth, rows // height
    places = block_planes * block_rows
    dims = (planes, rows, cols, depth, height, bricks, n, nv, taps_z, taps_l)
    vmem = pl.BlockSpec(memory_space=pltpu.VMEM)
    dma = pltpu.SemaphoreType.DMA
    operands = (
        estimate.reshape(planes * rows, cols),
        raw_bricks.reshape(bricks * cells, cols),
        brick_slab.reshape(1, bricks),
        brick_pos,
        off_z, frac_z, off_y, frac_y, off_x, frac_x, psf_z, psf_y, psf_x,
    )
    return pl.pallas_call(
        functools.partial(step, dims),
        out_shape=jax.ShapeDtypeStruct((planes, share, cols), F32),
        in_specs=[pl.BlockSpec(memory_space=pltpu.HBM)] * 13,
        out_specs=vmem,
        scratch_shapes=[pltpu.VMEM(o.shape, o.dtype) for o in operands] + [
            dma((13,)),
            pltpu.VMEM((rows, 3 * planes, cols), BF16),
            pltpu.VMEM((rows, 3 * planes, cols), BF16),
            pltpu.VMEM((max(rows * planes, bricks * cells), cols), F32),
            pltpu.VMEM((planes, rows, cols), F32),
            pltpu.VMEM((block_planes, depth, height, block_rows, cols), F32),
            pltpu.VMEM((wide, wide), BF16),
            pltpu.VMEM((bricks, wide), BF16),
            pltpu.VMEM((bricks, wide), BF16),
            pltpu.VMEM((slots, wide), BF16),
            pltpu.VMEM((slots, wide), BF16),
            pltpu.VMEM((n, 16, 128), BF16),
            pltpu.VMEM((n, 16, 128), BF16),
            pltpu.VMEM((8, slots), F32),
            pltpu.VMEM((places, slots), BF16),
            pltpu.VMEM((planes, rows, cols), BF16),
            pltpu.VMEM((nv, planes, share, cols), BF16),
            pltpu.VMEM((nv, cols, cols), BF16),
            pltpu.VMEM((1, bricks), jnp.int32),
            dma((2, CHUNKS)),
            dma((2, CHUNKS)),
            dma((2, 2)),
            dma((2, 2)),
            dma((nv, 2, 2)),
            dma((nv, 2, 2)),
            dma((n,)),
            dma((n,)),
            dma((n,)),
            dma((n,)),
            dma((nv, CHUNKS)),
            dma((nv, CHUNKS)),
            dma((nv,)),
            dma((nv,)),
            dma((2,)),
        ],
        compiler_params=pltpu.CompilerParams(
            collective_id=0, has_side_effects=True, vmem_limit_bytes=63 * 1024 * 1024
        ),
    )(*operands)


def solution(mesh):
    in_specs = (
        P("gz", None, None),
        P("view", "gz", None, None, None),
        P("view", "gz", None),
        P("view", "gz"),
    ) + (P("view", None),) * 9
    out_specs = P("gz", "view", None)
    return jax.shard_map(shards, mesh=mesh, in_specs=in_specs, out_specs=out_specs, check_vma=False)
```

```python
import functools

import jax
import jax.numpy as jnp
from jax import lax
from jax.experimental import pallas as pl
from jax.experimental.pallas import tpu as pltpu
from jax.sharding import PartitionSpec as P

BF16 = jnp.bfloat16
F32 = jnp.float32
CHUNKS = 4


def iota(shape, dim):
    return lax.broadcasted_iota(jnp.int32, shape, dim)


def tap_table(psf, count, which):
    normed = psf[...] / jnp.sum(psf[...], axis=1, keepdims=True)
    table = jnp.zeros(which.shape, F32)
    for k in range(count):
        table = jnp.where(which == k, jnp.broadcast_to(normed[0:1, k:k + 1], which.shape), table)
    return table.astype(BF16)


def small_weight(off, frac, column, source):
    fraction = jnp.broadcast_to(frac[0:1, column:column + 1], (1, 128))
    offset = jnp.broadcast_to(off[0:1, column:column + 1], (1, 128))
    low = (1.0 - fraction).astype(BF16).astype(F32)
    high = fraction.astype(BF16).astype(F32)
    return jnp.where(offset == source, low, 0.0) + jnp.where(offset + 1 == source, high, 0.0)


def step(
    dims,
    *refs,
):
    operands, out, fetched, fetch_sem = refs[:13], refs[13], refs[14:27], refs[27]
    est, raw, slab, pos, off_z, frac_z, off_y, frac_y, off_x, frac_x, psf_z, psf_y, psf_x = fetched
    body(
        dims, operands, fetched, fetch_sem,
        est, raw, slab, pos, off_z, frac_z, off_y, frac_y, off_x, frac_x, psf_z, psf_y, psf_x,
        out, *refs[28:],
    )


def body(
    dims, operands, fetched, fetch_sem,
    est, raw, slab, pos, off_z, frac_z, off_y, frac_y, off_x, frac_x, psf_z, psf_y, psf_x,
    out,
    pad1, pad2, work, blurred, joined, weights, by_cell, mixed, outgoing, arrived, pos_out, pos_in, pos_row,
    placer, back_y, back, from_views, x_tables, slot_scr,
    halo_send, halo_recv, share_send, share_recv, pass_send, pass_recv, brick_send, brick_recv, pos_send, pos_recv, view_send, view_recv,
    xt_send, xt_recv, own_sem,
):
    planes, rows, cols, depth, height, bricks, n, nv, taps_z, taps_l = dims
    cells = depth * height
    wide = cells * cols
    cap = max(2, 2 * bricks // n)
    slots = n * cap
    block_planes = planes // depth
    block_rows = rows // height
    places = block_planes * block_rows
    half = taps_z // 2
    lat = taps_l // 2
    share = rows // nv
    zpart = planes // CHUNKS
    piece = share // 2
    me = lax.axis_index("gz")
    mv = lax.axis_index("view")

    fetches = [
        pltpu.make_async_copy(operands[i], fetched[i], fetch_sem.at[i]) for i in range(len(operands))
    ]
    for fetch in fetches:
        fetch.start()

    barrier = pltpu.get_barrier_semaphore()

    @pl.loop(1, n)
    def _(i):
        pl.semaphore_signal(barrier, inc=1, device_id={"gz": lax.rem(me + i, n)})

    @pl.loop(1, nv)
    def _(i):
        pl.semaphore_signal(barrier, inc=1, device_id={"view": lax.rem(mv + i, nv)})

    def own_rows(source, pad, start, count):
        @pl.loop(0, count, unroll=8)
        def _(i):
            y = start + i
            pad[y, pl.ds(planes, planes), :] = source[pl.ds(y, planes, stride=rows), :].astype(BF16)

    fetches[0].wait()
    own_rows(est, pad1, 0, rows)

    pl.semaphore_wait(barrier, n - 1 + nv - 1)

    left, right = lax.rem(me + n - 1, n), lax.rem(me + 1, n)

    def neighbours(start_row, count, pad, send_sems, recv_sems, c):
        def copy(side):
            return pltpu.make_async_remote_copy(
                src_ref=pad.at[pl.ds(start_row, count), pl.ds(planes, planes), :],
                dst_ref=pad.at[pl.ds(start_row, count), pl.ds(side * 2 * planes, planes), :],
                send_sem=send_sems.at[side, c],
                recv_sem=recv_sems.at[side, c],
                device_id={"gz": (right, left)[side]},
                device_id_type=pl.DeviceIdType.MESH,
            )

        return copy

    def on_sides(to_right, to_left, arriving=False):
        @pl.when(me > 0 if arriving else me < n - 1)
        def _():
            to_right()

        @pl.when(me < n - 1 if arriving else me > 0)
        def _():
            to_left()

    def share_copy(c):
        return neighbours(mv * share + c * piece, piece, pad1, share_send, share_recv, c)

    def pass_copy(side, c, peer, owner):
        block = pad1.at[pl.ds(owner * share + c * piece, piece), pl.ds(side * 2 * planes, planes), :]
        return pltpu.make_async_remote_copy(
            src_ref=block,
            dst_ref=block,
            send_sem=pass_send.at[peer, side, c],
            recv_sem=pass_recv.at[owner, side, c],
            device_id={"view": peer},
            device_id_type=pl.DeviceIdType.MESH,
        )

    if nv == 2 and lat <= 16 and share > 16:
        lead = (share + 16) // height
        rest = block_rows - lead
        segments = [(d, (1 - mv) * rest, lead) for d in range(height)]
        later = [(d, mv * lead, rest) for d in range(height)]
    else:
        segments = [(d, 0, block_rows) for d in range(height)]
        later = []

    def segment_start(d, at):
        return pl.multiple_of(d * block_rows + at, 8)

    def halo(c):
        d, at, count = (segments + later)[c]
        return neighbours(segment_start(d, at), count, pad2, halo_send, halo_recv, c)

    for c in range(2):
        copy = share_copy(c)
        on_sides(copy(0).start, copy(1).start)

    @pl.when(me == 0)
    def _():
        for pad in (pad1, pad2):
            pad[:, pl.ds(0, planes), :] = jnp.zeros((rows, planes, cols), BF16)

    @pl.when(me == n - 1)
    def _():
        for pad in (pad1, pad2):
            pad[:, pl.ds(2 * planes, planes), :] = jnp.zeros((rows, planes, cols), BF16)

    for fetch in fetches[1:]:
        fetch.wait()
    source = iota((cols, cols), 0)
    low = (1.0 - frac_x[...]).astype(BF16).astype(F32)
    high = frac_x[...].astype(BF16).astype(F32)
    along = jnp.where(source == off_x[...], low, 0.0) + jnp.where(source == off_x[...] + 1, high, 0.0)
    along_b = along.astype(BF16)
    quarter = bricks * cells // 4
    for i in range(4):
        work[i * quarter:(i + 1) * quarter, :] = jnp.dot(
            raw[i * quarter:(i + 1) * quarter, :], along_b, preferred_element_type=F32
        ).astype(BF16).astype(F32)
    for q in range(cells):
        by_cell[:, q * cols:(q + 1) * cols] = work[pl.ds(q, bricks, stride=cells), :].astype(BF16)
    unit = (iota((cols, cols), 0) == iota((cols, cols), 1)).astype(F32)
    for a in range(depth):
        for c in range(depth):
            wz = small_weight(off_z, frac_z, c, a)
            for e in range(height):
                for d in range(height):
                    wy = small_weight(off_y, frac_y, d, e)
                    weights[
                        (a * height + e) * cols:(a * height + e + 1) * cols,
                        (c * height + d) * cols:(c * height + d + 1) * cols,
                    ] = (unit * (wz * wy)).astype(BF16)
    for i in range(wide // 256):
        mixed[:, i * 256:(i + 1) * 256] = jnp.dot(
            by_cell[...], weights[:, i * 256:(i + 1) * 256], preferred_element_type=F32
        ).astype(BF16)

    slab_v = slab[...]
    member = iota((n, bricks), 0) == slab_v
    before = (iota((bricks, bricks), 0) < iota((bricks, bricks), 1)).astype(F32).astype(BF16)
    earlier = jnp.dot(member.astype(F32).astype(BF16), before, preferred_element_type=F32)
    order = jnp.sum(jnp.where(member, earlier, 0.0), axis=0, keepdims=True).astype(jnp.int32)
    slot_scr[...] = slab_v * cap + order
    pos_v = pos[...]
    row16 = iota((16, bricks), 0)
    pos_pair = jnp.where(
        row16 == 0, pos_v // 64 + 1, jnp.where(row16 == 1, lax.rem(pos_v, 64), 0)
    ).astype(F32).astype(BF16)
    for i in range(slots // 256):
        chosen = ((iota((256, bricks), 0) + i * 256) == slot_scr[...]).astype(F32).astype(BF16)
        outgoing[i * 256:(i + 1) * 256, :] = jnp.dot(
            chosen, mixed[...], preferred_element_type=F32
        ).astype(BF16)
        slot_pos = lax.dot_general(
            pos_pair, chosen, (((1,), (1,)), ((), ())), preferred_element_type=F32
        )
        for j in range(256 // cap):
            pos_out[i * (256 // cap) + j, :, 0:cap] = slot_pos[:, j * cap:(j + 1) * cap].astype(BF16)

    def brick_copy(peer, owner):
        return pltpu.make_async_remote_copy(
            src_ref=outgoing.at[pl.ds(pl.multiple_of(peer * cap, cap), cap), :],
            dst_ref=arrived.at[pl.ds(pl.multiple_of(owner * cap, cap), cap), :],
            send_sem=brick_send.at[peer],
            recv_sem=brick_recv.at[owner],
            device_id={"gz": peer},
            device_id_type=pl.DeviceIdType.MESH,
        )

    def pos_copy(peer, owner):
        return pltpu.make_async_remote_copy(
            src_ref=pos_out.at[peer],
            dst_ref=pos_in.at[owner],
            send_sem=pos_send.at[peer],
            recv_sem=pos_recv.at[owner],
            device_id={"gz": peer},
            device_id_type=pl.DeviceIdType.MESH,
        )

    @pl.loop(1, n)
    def _(i):
        peer = lax.rem(me + i, n)
        brick_copy(peer, me).start()
        pos_copy(peer, me).start()

    mine = pl.ds(pl.multiple_of(me * cap, cap), cap)
    own_bricks = pltpu.make_async_copy(outgoing.at[mine, :], arrived.at[mine, :], own_sem.at[0])
    own_pos = pltpu.make_async_copy(pos_out.at[me], pos_in.at[me], own_sem.at[1])
    own_bricks.start()
    own_pos.start()

    def true_row(r):
        return lax.rem(r, block_rows) * height + r // block_rows

    ii, jj = iota((rows, rows), 0), iota((rows, rows), 1)
    fy = tap_table(psf_y, taps_l, jj - true_row(ii) + lat)
    back_y[...] = tap_table(psf_y, taps_l, ii - true_row(jj) + lat)
    ci, cj = iota((cols, cols), 0), iota((cols, cols), 1)
    fx = tap_table(psf_x, taps_l, ci - cj + lat)
    x_tables[mv] = tap_table(psf_x, taps_l, cj - ci + lat)
    zi, zj = iota((planes, 3 * planes), 0), iota((planes, 3 * planes), 1)
    fz = tap_table(psf_z, taps_z, zj - zi - (planes - half))
    bz = tap_table(psf_z, taps_z, planes + half + zi - zj)

    def xt_copy(peer, owner):
        return pltpu.make_async_remote_copy(
            src_ref=x_tables.at[mv],
            dst_ref=x_tables.at[owner],
            send_sem=xt_send.at[peer],
            recv_sem=xt_recv.at[owner],
            device_id={"view": peer},
            device_id_type=pl.DeviceIdType.MESH,
        )

    @pl.loop(1, nv)
    def _(i):
        xt_copy(lax.rem(mv + i, nv), mv).start()

    def z_pass(pad, table, start, count):
        @pl.loop(0, count // 4, unroll=2)
        def _(i):
            y = start + i * 4
            block = jnp.concatenate([pad[y + j] for j in range(4)], axis=1)
            result = jnp.dot(table, block, preferred_element_type=F32)
            result = result.astype(BF16).astype(F32)
            for j in range(4):
                work[pl.ds((y + j) * planes, planes), :] = result[:, j * cols:(j + 1) * cols]

    def y_pass(table, z):
        block = jnp.concatenate(
            [work[pl.ds(z + j, rows, stride=planes), :].astype(BF16) for j in range(2)], axis=1
        )
        return jnp.dot(table, block, preferred_element_type=F32).astype(BF16)

    def pass_on(side, c):
        @pl.loop(1, nv)
        def _(i):
            pass_copy(side, c, lax.rem(mv + i, nv), mv).start()

    def pass_take(side, c, owner):
        pass_copy(side, c, mv, owner).wait_recv()

    def pass_sent(side, c):
        @pl.loop(1, nv)
        def _(i):
            pass_copy(side, c, lax.rem(mv + i, nv), mv).wait_send()

    for c in range(2):
        copy = share_copy(c)
        on_sides(copy(0).wait_recv, copy(1).wait_recv, arriving=True)
        on_sides(lambda: pass_on(0, c), lambda: pass_on(1, c), arriving=True)
    z_pass(pad1, fz, mv * share, share)
    for v in range(1, nv):
        owner = lax.rem(mv + nv - v, nv)
        for c in range(2):
            on_sides(lambda: pass_take(0, c, owner), lambda: pass_take(1, c, owner), arriving=True)
            z_pass(pad1, fz, owner * share + c * piece, piece)

    @pl.loop(0, planes // 2, unroll=4)
    def _(i):
        along_y = y_pass(fy, 2 * i)
        for j in range(2):
            blurred[2 * i + j] = jnp.dot(
                along_y[:, j * cols:(j + 1) * cols], fx, preferred_element_type=F32
            )

    own_pos.wait()

    @pl.loop(1, n)
    def _(i):
        pos_copy(me, lax.rem(me + n - i, n)).wait_recv()

    for s in range(n):
        pair = pos_in[s].astype(F32)
        pos_row[0:1, s * cap:(s + 1) * cap] = ((pair[0:1] - 1.0) * 64.0 + pair[1:2])[:, 0:cap]
    for i in range(places // 128):
        place = (iota((128, slots), 0) + i * 128).astype(F32)
        placer[i * 128:(i + 1) * 128, :] = (place == pos_row[0:1, :]).astype(F32).astype(BF16)

    own_bricks.wait()

    @pl.loop(1, n)
    def _(i):
        brick_copy(me, lax.rem(me + n - i, n)).wait_recv()

    for c in range(depth):
        for d in range(height):
            at = (c * height + d) * cols
            if d % 2 == 0:
                added = jnp.dot(placer[...], arrived[:, at:at + 2 * cols], preferred_element_type=F32)
            joined[:, c, d, :, :] = added[:, (d % 2) * cols:(d % 2 + 1) * cols].reshape(
                block_planes, block_rows, cols
            )

    for c, (d, at, count) in enumerate(segments + later):
        start = segment_start(d, at)

        @pl.loop(0, block_planes)
        def _(i):
            for k in range(depth):
                z = i * depth + k
                work[pl.ds(pl.multiple_of(z * rows + start, 8), count), :] = (
                    1.0 + joined[i, k, d, pl.ds(pl.multiple_of(at, 8), count), :]
                ) / blurred[z, pl.ds(start, count), :]

        own_rows(work, pad2, start, count)
        copy = halo(c)
        on_sides(copy(0).start, copy(1).start)

    def arrive(c):
        d, at, count = (segments + later)[c]
        copy = halo(c)
        on_sides(copy(0).wait_recv, copy(1).wait_recv, arriving=True)
        z_pass(pad2, bz, segment_start(d, at), count)

    def back_rows(view, z):
        at = pl.multiple_of(view * share, share)
        along_y = y_pass(back_y[pl.ds(at, share), :], z)
        for j in range(2):
            back[z + j, pl.ds(at, share), :] = along_y[:, j * cols:(j + 1) * cols]

    for c in range(len(segments)):
        arrive(c)

    def view_copy(peer, owner, c):
        return pltpu.make_async_remote_copy(
            src_ref=back.at[pl.ds(c * zpart, zpart), pl.ds(pl.multiple_of(peer * share, share), share), :],
            dst_ref=from_views.at[owner, pl.ds(c * zpart, zpart), :, :],
            send_sem=view_send.at[peer, c],
            recv_sem=view_recv.at[owner, c],
            device_id={"view": peer},
            device_id_type=pl.DeviceIdType.MESH,
        )

    for c in range(CHUNKS):
        for v in range(1, nv):
            peer = lax.rem(mv + v, nv)

            @pl.loop(0, zpart // 2, unroll=4)
            def _(i):
                back_rows(peer, c * zpart + 2 * i)

            view_copy(peer, mv, c).start()

    for c in range(len(later)):
        arrive(len(segments) + c)

    @pl.loop(0, planes // 2, unroll=4)
    def _(i):
        back_rows(mv, 2 * i)

    first = pl.multiple_of(mv * share, share)

    @pl.loop(1, nv)
    def _(i):
        xt_copy(mv, lax.rem(mv + i, nv)).wait_recv()

    for c in range(CHUNKS):
        @pl.loop(1, nv)
        def _(i):
            view_copy(mv, lax.rem(mv + i, nv), c).wait_recv()

        planes_c = slice(c * zpart, (c + 1) * zpart)
        total = jnp.dot(
            back[planes_c, pl.ds(first, share), :].reshape(zpart * share, cols),
            x_tables[mv],
            preferred_element_type=F32,
        )
        for v in range(1, nv):
            other = lax.rem(mv + v, nv)
            total = total + jnp.dot(
                from_views[other, planes_c].reshape(zpart * share, cols),
                x_tables[other],
                preferred_element_type=F32,
            )
        for k in range(zpart):
            z = c * zpart + k
            out[z] = (
                est[pl.ds(pl.multiple_of(z * rows + first, share), share), :]
                * total[k * share:(k + 1) * share]
                * (1.0 / nv)
            )

    for c in range(2):
        copy = share_copy(c)
        on_sides(copy(0).wait_send, copy(1).wait_send)
        on_sides(lambda: pass_sent(0, c), lambda: pass_sent(1, c), arriving=True)
    for c in range(len(segments + later)):
        copy = halo(c)
        on_sides(copy(0).wait_send, copy(1).wait_send)
    for c in range(CHUNKS):
        @pl.loop(1, nv)
        def _(i):
            view_copy(lax.rem(mv + i, nv), mv, c).wait_send()

    @pl.loop(1, nv)
    def _(i):
        xt_copy(lax.rem(mv + i, nv), mv).wait_send()

    @pl.loop(1, n)
    def _(i):
        peer = lax.rem(me + i, n)
        brick_copy(peer, me).wait_send()
        pos_copy(peer, me).wait_send()


def shards(
    estimate, raw_bricks, brick_slab, brick_pos, off_z, frac_z, off_y, frac_y, off_x, frac_x,
    psf_z, psf_y, psf_x,
):
    planes, rows, cols = estimate.shape
    _, bricks, depth, height, _ = raw_bricks.shape
    n, nv = lax.axis_size("gz"), lax.axis_size("view")
    taps_z, taps_l = psf_z.shape[1], psf_x.shape[1]
    cells = depth * height
    wide = cells * cols
    cap = max(2, 2 * bricks // n)
    slots = n * cap
    share = rows // nv
    block_planes, block_rows = planes // depth, rows // height
    places = block_planes * block_rows
    dims = (planes, rows, cols, depth, height, bricks, n, nv, taps_z, taps_l)
    vmem = pl.BlockSpec(memory_space=pltpu.VMEM)
    dma = pltpu.SemaphoreType.DMA
    operands = (
        estimate.reshape(planes * rows, cols),
        raw_bricks.reshape(bricks * cells, cols),
        brick_slab.reshape(1, bricks),
        brick_pos,
        off_z, frac_z, off_y, frac_y, off_x, frac_x, psf_z, psf_y, psf_x,
    )
    return pl.pallas_call(
        functools.partial(step, dims),
        out_shape=jax.ShapeDtypeStruct((planes, share, cols), F32),
        in_specs=[pl.BlockSpec(memory_space=pltpu.HBM)] * 13,
        out_specs=vmem,
        scratch_shapes=[pltpu.VMEM(o.shape, o.dtype) for o in operands] + [
            dma((13,)),
            pltpu.VMEM((rows, 3 * planes, cols), BF16),
            pltpu.VMEM((rows, 3 * planes, cols), BF16),
            pltpu.VMEM((max(rows * planes, bricks * cells), cols), F32),
            pltpu.VMEM((planes, rows, cols), F32),
            pltpu.VMEM((block_planes, depth, height, block_rows, cols), F32),
            pltpu.VMEM((wide, wide), BF16),
            pltpu.VMEM((bricks, wide), BF16),
            pltpu.VMEM((bricks, wide), BF16),
            pltpu.VMEM((slots, wide), BF16),
            pltpu.VMEM((slots, wide), BF16),
            pltpu.VMEM((n, 16, 128), BF16),
            pltpu.VMEM((n, 16, 128), BF16),
            pltpu.VMEM((8, slots), F32),
            pltpu.VMEM((places, slots), BF16),
            pltpu.VMEM((rows, rows), BF16),
            pltpu.VMEM((planes, rows, cols), BF16),
            pltpu.VMEM((nv, planes, share, cols), BF16),
            pltpu.VMEM((nv, cols, cols), BF16),
            pltpu.VMEM((1, bricks), jnp.int32),
            dma((2, 2 * height)),
            dma((2, 2 * height)),
            dma((2, 2)),
            dma((2, 2)),
            dma((nv, 2, 2)),
            dma((nv, 2, 2)),
            dma((n,)),
            dma((n,)),
            dma((n,)),
            dma((n,)),
            dma((nv, CHUNKS)),
            dma((nv, CHUNKS)),
            dma((nv,)),
            dma((nv,)),
            dma((2,)),
        ],
        compiler_params=pltpu.CompilerParams(
            collective_id=0, has_side_effects=True, vmem_limit_bytes=63 * 1024 * 1024
        ),
    )(*operands)


def solution(mesh):
    in_specs = (
        P("gz", None, None),
        P("view", "gz", None, None, None),
        P("view", "gz", None),
        P("view", "gz"),
    ) + (P("view", None),) * 9
    out_specs = P("gz", "view", None)
    return jax.shard_map(shards, mesh=mesh, in_specs=in_specs, out_specs=out_specs, check_vma=False)
```

```python
import functools

import jax
import jax.numpy as jnp
from jax import lax
from jax.experimental import pallas as pl
from jax.experimental.pallas import tpu as pltpu
from jax.sharding import PartitionSpec as P

BF16 = jnp.bfloat16
F32 = jnp.float32
CHUNKS = 4


def iota(shape, dim):
    return lax.broadcasted_iota(jnp.int32, shape, dim)


def tap_table(psf, count, which):
    normed = psf[...] / jnp.sum(psf[...], axis=1, keepdims=True)
    table = jnp.zeros(which.shape, F32)
    for k in range(count):
        table = jnp.where(which == k, jnp.broadcast_to(normed[0:1, k:k + 1], which.shape), table)
    return table.astype(BF16)


def small_weight(off, frac, column, source):
    fraction = jnp.broadcast_to(frac[0:1, column:column + 1], (1, 128))
    offset = jnp.broadcast_to(off[0:1, column:column + 1], (1, 128))
    low = (1.0 - fraction).astype(BF16).astype(F32)
    high = fraction.astype(BF16).astype(F32)
    return jnp.where(offset == source, low, 0.0) + jnp.where(offset + 1 == source, high, 0.0)


def step(
    dims,
    *refs,
):
    operands, out, fetched, fetch_sem = refs[:13], refs[13], refs[14:27], refs[27]
    est, raw, slab, pos, off_z, frac_z, off_y, frac_y, off_x, frac_x, psf_z, psf_y, psf_x = fetched
    body(
        dims, operands, fetched, fetch_sem,
        est, raw, slab, pos, off_z, frac_z, off_y, frac_y, off_x, frac_x, psf_z, psf_y, psf_x,
        out, *refs[28:],
    )


def body(
    dims, operands, fetched, fetch_sem,
    est, raw, slab, pos, off_z, frac_z, off_y, frac_y, off_x, frac_x, psf_z, psf_y, psf_x,
    out,
    pad1, pad2, work, inverse, joined, weights, by_cell, mixed, outgoing, arrived, pos_out, pos_in, pos_row,
    placer, back_y, back, from_views, x_tables, slot_scr,
    halo_send, halo_recv, share_send, share_recv, pass_send, pass_recv, brick_send, brick_recv, pos_send, pos_recv, view_send, view_recv,
    xt_send, xt_recv, own_sem,
):
    planes, rows, cols, depth, height, bricks, n, nv, taps_z, taps_l = dims
    cells = depth * height
    wide = cells * cols
    cap = max(2, 2 * bricks // n)
    slots = n * cap
    block_planes = planes // depth
    block_rows = rows // height
    places = block_planes * block_rows
    half = taps_z // 2
    lat = taps_l // 2
    share = rows // nv
    zpart = planes // CHUNKS
    piece = share // 2
    me = lax.axis_index("gz")
    mv = lax.axis_index("view")

    fetches = [
        pltpu.make_async_copy(operands[i], fetched[i], fetch_sem.at[i]) for i in range(len(operands))
    ]
    for fetch in fetches:
        fetch.start()

    barrier = pltpu.get_barrier_semaphore()

    @pl.loop(1, n)
    def _(i):
        pl.semaphore_signal(barrier, inc=1, device_id={"gz": lax.rem(me + i, n)})

    @pl.loop(1, nv)
    def _(i):
        pl.semaphore_signal(barrier, inc=1, device_id={"view": lax.rem(mv + i, nv)})

    def own_rows(source, pad, start, count):
        @pl.loop(0, count, unroll=8)
        def _(i):
            y = start + i
            pad[y, pl.ds(planes, planes), :] = source[pl.ds(y, planes, stride=rows), :].astype(BF16)

    fetches[0].wait()
    own_rows(est, pad1, 0, rows)

    pl.semaphore_wait(barrier, n - 1 + nv - 1)

    left, right = lax.rem(me + n - 1, n), lax.rem(me + 1, n)

    def neighbours(start_row, count, pad, send_sems, recv_sems, c):
        def copy(side):
            return pltpu.make_async_remote_copy(
                src_ref=pad.at[pl.ds(start_row, count), pl.ds(planes, planes), :],
                dst_ref=pad.at[pl.ds(start_row, count), pl.ds(side * 2 * planes, planes), :],
                send_sem=send_sems.at[side, c],
                recv_sem=recv_sems.at[side, c],
                device_id={"gz": (right, left)[side]},
                device_id_type=pl.DeviceIdType.MESH,
            )

        return copy

    def on_sides(to_right, to_left, arriving=False):
        @pl.when(me > 0 if arriving else me < n - 1)
        def _():
            to_right()

        @pl.when(me < n - 1 if arriving else me > 0)
        def _():
            to_left()

    def share_copy(c):
        return neighbours(mv * share + c * piece, piece, pad1, share_send, share_recv, c)

    def pass_copy(side, c, peer, owner):
        block = pad1.at[pl.ds(owner * share + c * piece, piece), pl.ds(side * 2 * planes, planes), :]
        return pltpu.make_async_remote_copy(
            src_ref=block,
            dst_ref=block,
            send_sem=pass_send.at[peer, side, c],
            recv_sem=pass_recv.at[owner, side, c],
            device_id={"view": peer},
            device_id_type=pl.DeviceIdType.MESH,
        )

    if nv == 2 and lat <= 16 and share > 16:
        lead = (share + 16) // height
        rest = block_rows - lead
        segments = [(d, (1 - mv) * rest, lead) for d in range(height)]
        later = [(d, mv * lead, rest) for d in range(height)]
    else:
        segments = [(d, 0, block_rows) for d in range(height)]
        later = []

    def segment_start(d, at):
        return pl.multiple_of(d * block_rows + at, 8)

    def halo(c):
        d, at, count = (segments + later)[c]
        return neighbours(segment_start(d, at), count, pad2, halo_send, halo_recv, c)

    for c in range(2):
        copy = share_copy(c)
        on_sides(copy(0).start, copy(1).start)

    @pl.when(me == 0)
    def _():
        for pad in (pad1, pad2):
            pad[:, pl.ds(0, planes), :] = jnp.zeros((rows, planes, cols), BF16)

    @pl.when(me == n - 1)
    def _():
        for pad in (pad1, pad2):
            pad[:, pl.ds(2 * planes, planes), :] = jnp.zeros((rows, planes, cols), BF16)

    for fetch in fetches[1:]:
        fetch.wait()
    source = iota((cols, cols), 0)
    low = (1.0 - frac_x[...]).astype(BF16).astype(F32)
    high = frac_x[...].astype(BF16).astype(F32)
    along = jnp.where(source == off_x[...], low, 0.0) + jnp.where(source == off_x[...] + 1, high, 0.0)
    along_b = along.astype(BF16)
    quarter = bricks * cells // 4
    for i in range(4):
        work[i * quarter:(i + 1) * quarter, :] = jnp.dot(
            raw[i * quarter:(i + 1) * quarter, :], along_b, preferred_element_type=F32
        ).astype(BF16).astype(F32)
    for q in range(cells):
        by_cell[:, q * cols:(q + 1) * cols] = work[pl.ds(q, bricks, stride=cells), :].astype(BF16)
    unit = (iota((cols, cols), 0) == iota((cols, cols), 1)).astype(F32)
    for a in range(depth):
        for c in range(depth):
            wz = small_weight(off_z, frac_z, c, a)
            for e in range(height):
                for d in range(height):
                    wy = small_weight(off_y, frac_y, d, e)
                    weights[
                        (a * height + e) * cols:(a * height + e + 1) * cols,
                        (c * height + d) * cols:(c * height + d + 1) * cols,
                    ] = (unit * (wz * wy)).astype(BF16)
    for i in range(wide // 256):
        mixed[:, i * 256:(i + 1) * 256] = jnp.dot(
            by_cell[...], weights[:, i * 256:(i + 1) * 256], preferred_element_type=F32
        ).astype(BF16)

    slab_v = slab[...]
    member = iota((n, bricks), 0) == slab_v
    before = (iota((bricks, bricks), 0) < iota((bricks, bricks), 1)).astype(F32).astype(BF16)
    earlier = jnp.dot(member.astype(F32).astype(BF16), before, preferred_element_type=F32)
    order = jnp.sum(jnp.where(member, earlier, 0.0), axis=0, keepdims=True).astype(jnp.int32)
    slot_scr[...] = slab_v * cap + order
    pos_v = pos[...]
    row16 = iota((16, bricks), 0)
    pos_pair = jnp.where(
        row16 == 0, pos_v // 64 + 1, jnp.where(row16 == 1, lax.rem(pos_v, 64), 0)
    ).astype(F32).astype(BF16)
    for i in range(slots // 256):
        chosen = ((iota((256, bricks), 0) + i * 256) == slot_scr[...]).astype(F32).astype(BF16)
        outgoing[i * 256:(i + 1) * 256, :] = jnp.dot(
            chosen, mixed[...], preferred_element_type=F32
        ).astype(BF16)
        slot_pos = lax.dot_general(
            pos_pair, chosen, (((1,), (1,)), ((), ())), preferred_element_type=F32
        )
        for j in range(256 // cap):
            pos_out[i * (256 // cap) + j, :, 0:cap] = slot_pos[:, j * cap:(j + 1) * cap].astype(BF16)

    def brick_copy(peer, owner):
        return pltpu.make_async_remote_copy(
            src_ref=outgoing.at[pl.ds(pl.multiple_of(peer * cap, cap), cap), :],
            dst_ref=arrived.at[pl.ds(pl.multiple_of(owner * cap, cap), cap), :],
            send_sem=brick_send.at[peer],
            recv_sem=brick_recv.at[owner],
            device_id={"gz": peer},
            device_id_type=pl.DeviceIdType.MESH,
        )

    def pos_copy(peer, owner):
        return pltpu.make_async_remote_copy(
            src_ref=pos_out.at[peer],
            dst_ref=pos_in.at[owner],
            send_sem=pos_send.at[peer],
            recv_sem=pos_recv.at[owner],
            device_id={"gz": peer},
            device_id_type=pl.DeviceIdType.MESH,
        )

    @pl.loop(1, n)
    def _(i):
        pos_copy(lax.rem(me + i, n), me).start()

    @pl.loop(1, n)
    def _(i):
        brick_copy(lax.rem(me + i, n), me).start()

    mine = pl.ds(pl.multiple_of(me * cap, cap), cap)
    own_bricks = pltpu.make_async_copy(outgoing.at[mine, :], arrived.at[mine, :], own_sem.at[0])
    own_pos = pltpu.make_async_copy(pos_out.at[me], pos_in.at[me], own_sem.at[1])
    own_bricks.start()
    own_pos.start()

    def true_row(r):
        return lax.rem(r, block_rows) * height + r // block_rows

    ii, jj = iota((rows, rows), 0), iota((rows, rows), 1)
    fy = tap_table(psf_y, taps_l, jj - true_row(ii) + lat)
    back_y[...] = tap_table(psf_y, taps_l, ii - true_row(jj) + lat)
    ci, cj = iota((cols, cols), 0), iota((cols, cols), 1)
    fx = tap_table(psf_x, taps_l, ci - cj + lat)
    x_tables[mv] = tap_table(psf_x, taps_l, cj - ci + lat)
    zi, zj = iota((planes, 3 * planes), 0), iota((planes, 3 * planes), 1)
    fz = tap_table(psf_z, taps_z, zj - zi - (planes - half))
    bz = tap_table(psf_z, taps_z, planes + half + zi - zj)

    def xt_copy(peer, owner):
        return pltpu.make_async_remote_copy(
            src_ref=x_tables.at[mv],
            dst_ref=x_tables.at[owner],
            send_sem=xt_send.at[peer],
            recv_sem=xt_recv.at[owner],
            device_id={"view": peer},
            device_id_type=pl.DeviceIdType.MESH,
        )

    @pl.loop(1, nv)
    def _(i):
        xt_copy(lax.rem(mv + i, nv), mv).start()

    def z_pass(pad, table, start, count):
        @pl.loop(0, count // 4, unroll=2)
        def _(i):
            y = start + i * 4
            block = jnp.concatenate([pad[y + j] for j in range(4)], axis=1)
            result = jnp.dot(table, block, preferred_element_type=F32)
            result = result.astype(BF16).astype(F32)
            for j in range(4):
                work[pl.ds((y + j) * planes, planes), :] = result[:, j * cols:(j + 1) * cols]

    def y_pass(table, z):
        block = jnp.concatenate(
            [work[pl.ds(z + j, rows, stride=planes), :].astype(BF16) for j in range(2)], axis=1
        )
        return jnp.dot(table, block, preferred_element_type=F32).astype(BF16)

    def pass_on(side, c):
        @pl.loop(1, nv)
        def _(i):
            pass_copy(side, c, lax.rem(mv + i, nv), mv).start()

    def pass_take(side, c, owner):
        pass_copy(side, c, mv, owner).wait_recv()

    def pass_sent(side, c):
        @pl.loop(1, nv)
        def _(i):
            pass_copy(side, c, lax.rem(mv + i, nv), mv).wait_send()

    for c in range(2):
        copy = share_copy(c)
        on_sides(copy(0).wait_recv, copy(1).wait_recv, arriving=True)
        on_sides(lambda: pass_on(0, c), lambda: pass_on(1, c), arriving=True)
    z_pass(pad1, fz, mv * share, share)
    for v in range(1, nv):
        owner = lax.rem(mv + nv - v, nv)
        for c in range(2):
            on_sides(lambda: pass_take(0, c, owner), lambda: pass_take(1, c, owner), arriving=True)
            z_pass(pad1, fz, owner * share + c * piece, piece)

    @pl.loop(0, planes // 2, unroll=4)
    def _(i):
        along_y = y_pass(fy, 2 * i)
        for j in range(2):
            inverse[2 * i + j] = 1.0 / jnp.dot(
                along_y[:, j * cols:(j + 1) * cols], fx, preferred_element_type=F32
            )

    own_pos.wait()

    @pl.loop(1, n)
    def _(i):
        pos_copy(me, lax.rem(me + n - i, n)).wait_recv()

    for s in range(n):
        pair = pos_in[s].astype(F32)
        pos_row[0:1, s * cap:(s + 1) * cap] = ((pair[0:1] - 1.0) * 64.0 + pair[1:2])[:, 0:cap]
    for i in range(places // 128):
        place = (iota((128, slots), 0) + i * 128).astype(F32)
        placer[i * 128:(i + 1) * 128, :] = (place == pos_row[0:1, :]).astype(F32).astype(BF16)

    own_bricks.wait()

    @pl.loop(1, n)
    def _(i):
        brick_copy(me, lax.rem(me + n - i, n)).wait_recv()

    for c in range(depth):
        for d in range(height):
            at = (c * height + d) * cols
            if d % 2 == 0:
                added = jnp.dot(placer[...], arrived[:, at:at + 2 * cols], preferred_element_type=F32)
            joined[:, c, d, :, :] = added[:, (d % 2) * cols:(d % 2 + 1) * cols].reshape(
                block_planes, block_rows, cols
            )

    for c, (d, at, count) in enumerate(segments + later):
        start = segment_start(d, at)

        @pl.loop(0, block_planes)
        def _(i):
            for k in range(depth):
                z = i * depth + k
                work[pl.ds(pl.multiple_of(z * rows + start, 8), count), :] = (
                    1.0 + joined[i, k, d, pl.ds(pl.multiple_of(at, 8), count), :]
                ) * inverse[z, pl.ds(start, count), :]

        own_rows(work, pad2, start, count)
        copy = halo(c)
        on_sides(copy(0).start, copy(1).start)

    def arrive(c):
        d, at, count = (segments + later)[c]
        copy = halo(c)
        on_sides(copy(0).wait_recv, copy(1).wait_recv, arriving=True)
        z_pass(pad2, bz, segment_start(d, at), count)

    def back_rows(view, z):
        at = pl.multiple_of(view * share, share)
        along_y = y_pass(back_y[pl.ds(at, share), :], z)
        for j in range(2):
            back[z + j, pl.ds(at, share), :] = along_y[:, j * cols:(j + 1) * cols]

    for c in range(len(segments)):
        arrive(c)

    def view_copy(peer, owner, c):
        return pltpu.make_async_remote_copy(
            src_ref=back.at[pl.ds(c * zpart, zpart), pl.ds(pl.multiple_of(peer * share, share), share), :],
            dst_ref=from_views.at[owner, pl.ds(c * zpart, zpart), :, :],
            send_sem=view_send.at[peer, c],
            recv_sem=view_recv.at[owner, c],
            device_id={"view": peer},
            device_id_type=pl.DeviceIdType.MESH,
        )

    for c in range(CHUNKS):
        for v in range(1, nv):
            peer = lax.rem(mv + v, nv)

            @pl.loop(0, zpart // 2, unroll=4)
            def _(i):
                back_rows(peer, c * zpart + 2 * i)

            view_copy(peer, mv, c).start()

    for c in range(len(later)):
        arrive(len(segments) + c)

    @pl.loop(0, planes // 2, unroll=4)
    def _(i):
        back_rows(mv, 2 * i)

    first = pl.multiple_of(mv * share, share)

    @pl.loop(1, nv)
    def _(i):
        xt_copy(mv, lax.rem(mv + i, nv)).wait_recv()

    for c in range(CHUNKS):
        @pl.loop(1, nv)
        def _(i):
            view_copy(mv, lax.rem(mv + i, nv), c).wait_recv()

        planes_c = slice(c * zpart, (c + 1) * zpart)
        total = jnp.dot(
            back[planes_c, pl.ds(first, share), :].reshape(zpart * share, cols),
            x_tables[mv],
            preferred_element_type=F32,
        )
        for v in range(1, nv):
            other = lax.rem(mv + v, nv)
            total = total + jnp.dot(
                from_views[other, planes_c].reshape(zpart * share, cols),
                x_tables[other],
                preferred_element_type=F32,
            )
        for k in range(zpart):
            z = c * zpart + k
            out[z] = (
                est[pl.ds(pl.multiple_of(z * rows + first, share), share), :]
                * total[k * share:(k + 1) * share]
                * (1.0 / nv)
            )

    for c in range(2):
        copy = share_copy(c)
        on_sides(copy(0).wait_send, copy(1).wait_send)
        on_sides(lambda: pass_sent(0, c), lambda: pass_sent(1, c), arriving=True)
    for c in range(len(segments + later)):
        copy = halo(c)
        on_sides(copy(0).wait_send, copy(1).wait_send)
    for c in range(CHUNKS):
        @pl.loop(1, nv)
        def _(i):
            view_copy(lax.rem(mv + i, nv), mv, c).wait_send()

    @pl.loop(1, nv)
    def _(i):
        xt_copy(lax.rem(mv + i, nv), mv).wait_send()

    @pl.loop(1, n)
    def _(i):
        peer = lax.rem(me + i, n)
        brick_copy(peer, me).wait_send()
        pos_copy(peer, me).wait_send()


def shards(
    estimate, raw_bricks, brick_slab, brick_pos, off_z, frac_z, off_y, frac_y, off_x, frac_x,
    psf_z, psf_y, psf_x,
):
    planes, rows, cols = estimate.shape
    _, bricks, depth, height, _ = raw_bricks.shape
    n, nv = lax.axis_size("gz"), lax.axis_size("view")
    taps_z, taps_l = psf_z.shape[1], psf_x.shape[1]
    cells = depth * height
    wide = cells * cols
    cap = max(2, 2 * bricks // n)
    slots = n * cap
    share = rows // nv
    block_planes, block_rows = planes // depth, rows // height
    places = block_planes * block_rows
    dims = (planes, rows, cols, depth, height, bricks, n, nv, taps_z, taps_l)
    vmem = pl.BlockSpec(memory_space=pltpu.VMEM)
    dma = pltpu.SemaphoreType.DMA
    operands = (
        estimate.reshape(planes * rows, cols),
        raw_bricks.reshape(bricks * cells, cols),
        brick_slab.reshape(1, bricks),
        brick_pos,
        off_z, frac_z, off_y, frac_y, off_x, frac_x, psf_z, psf_y, psf_x,
    )
    return pl.pallas_call(
        functools.partial(step, dims),
        out_shape=jax.ShapeDtypeStruct((planes, share, cols), F32),
        in_specs=[pl.BlockSpec(memory_space=pltpu.HBM)] * 13,
        out_specs=vmem,
        scratch_shapes=[pltpu.VMEM(o.shape, o.dtype) for o in operands] + [
            dma((13,)),
            pltpu.VMEM((rows, 3 * planes, cols), BF16),
            pltpu.VMEM((rows, 3 * planes, cols), BF16),
            pltpu.VMEM((max(rows * planes, bricks * cells), cols), F32),
            pltpu.VMEM((planes, rows, cols), F32),
            pltpu.VMEM((block_planes, depth, height, block_rows, cols), F32),
            pltpu.VMEM((wide, wide), BF16),
            pltpu.VMEM((bricks, wide), BF16),
            pltpu.VMEM((bricks, wide), BF16),
            pltpu.VMEM((slots, wide), BF16),
            pltpu.VMEM((slots, wide), BF16),
            pltpu.VMEM((n, 16, 128), BF16),
            pltpu.VMEM((n, 16, 128), BF16),
            pltpu.VMEM((8, slots), F32),
            pltpu.VMEM((places, slots), BF16),
            pltpu.VMEM((rows, rows), BF16),
            pltpu.VMEM((planes, rows, cols), BF16),
            pltpu.VMEM((nv, planes, share, cols), BF16),
            pltpu.VMEM((nv, cols, cols), BF16),
            pltpu.VMEM((1, bricks), jnp.int32),
            dma((2, 2 * height)),
            dma((2, 2 * height)),
            dma((2, 2)),
            dma((2, 2)),
            dma((nv, 2, 2)),
            dma((nv, 2, 2)),
            dma((n,)),
            dma((n,)),
            dma((n,)),
            dma((n,)),
            dma((nv, CHUNKS)),
            dma((nv, CHUNKS)),
            dma((nv,)),
            dma((nv,)),
            dma((2,)),
        ],
        compiler_params=pltpu.CompilerParams(
            collective_id=0, has_side_effects=True, vmem_limit_bytes=63 * 1024 * 1024
        ),
    )(*operands)


def solution(mesh):
    in_specs = (
        P("gz", None, None),
        P("view", "gz", None, None, None),
        P("view", "gz", None),
        P("view", "gz"),
    ) + (P("view", None),) * 9
    out_specs = P("gz", "view", None)
    return jax.shard_map(shards, mesh=mesh, in_specs=in_specs, out_specs=out_specs, check_vma=False)
```

```python
import functools

import jax
import jax.numpy as jnp
from jax import lax
from jax.experimental import pallas as pl
from jax.experimental.pallas import tpu as pltpu
from jax.sharding import PartitionSpec as P

BF16 = jnp.bfloat16
F32 = jnp.float32
CHUNKS = 4


def iota(shape, dim):
    return lax.broadcasted_iota(jnp.int32, shape, dim)


def tap_table(psf, count, which):
    normed = psf[...] / jnp.sum(psf[...], axis=1, keepdims=True)
    table = jnp.zeros(which.shape, F32)
    for k in range(count):
        table = jnp.where(which == k, jnp.broadcast_to(normed[0:1, k:k + 1], which.shape), table)
    return table.astype(BF16)


def small_weight(off, frac, column, source):
    fraction = jnp.broadcast_to(frac[0:1, column:column + 1], (1, 128))
    offset = jnp.broadcast_to(off[0:1, column:column + 1], (1, 128))
    low = (1.0 - fraction).astype(BF16).astype(F32)
    high = fraction.astype(BF16).astype(F32)
    return jnp.where(offset == source, low, 0.0) + jnp.where(offset + 1 == source, high, 0.0)


def step(
    dims,
    *refs,
):
    operands, out, fetched, fetch_sem = refs[:13], refs[13], refs[14:27], refs[27]
    est, raw, slab, pos, off_z, frac_z, off_y, frac_y, off_x, frac_x, psf_z, psf_y, psf_x = fetched
    body(
        dims, operands, fetched, fetch_sem,
        est, raw, slab, pos, off_z, frac_z, off_y, frac_y, off_x, frac_x, psf_z, psf_y, psf_x,
        out, *refs[28:],
    )


def body(
    dims, operands, fetched, fetch_sem,
    est, raw, slab, pos, off_z, frac_z, off_y, frac_y, off_x, frac_x, psf_z, psf_y, psf_x,
    out,
    pad1, pad2, work, inverse, joined, weights, by_cell, mixed, outgoing, arrived, pos_out, pos_in, pos_row,
    placer, back_y, back, from_views, x_tables, slot_scr,
    halo_send, halo_recv, share_send, share_recv, pass_send, pass_recv, brick_send, brick_recv, pos_send, pos_recv, view_send, view_recv,
    xt_send, xt_recv, own_sem,
):
    planes, rows, cols, depth, height, bricks, n, nv, taps_z, taps_l = dims
    cells = depth * height
    wide = cells * cols
    cap = max(2, 2 * bricks // n)
    slots = n * cap
    block_planes = planes // depth
    block_rows = rows // height
    places = block_planes * block_rows
    half = taps_z // 2
    lat = taps_l // 2
    share = rows // nv
    zpart = planes // CHUNKS
    piece = share // 2
    me = lax.axis_index("gz")
    mv = lax.axis_index("view")

    fetches = [
        pltpu.make_async_copy(operands[i], fetched[i], fetch_sem.at[i]) for i in range(len(operands))
    ]
    for fetch in fetches:
        fetch.start()

    barrier = pltpu.get_barrier_semaphore()

    @pl.loop(1, n)
    def _(i):
        pl.semaphore_signal(barrier, inc=1, device_id={"gz": lax.rem(me + i, n)})

    @pl.loop(1, nv)
    def _(i):
        pl.semaphore_signal(barrier, inc=1, device_id={"view": lax.rem(mv + i, nv)})

    def own_rows(source, pad, start, count):
        @pl.loop(0, count, unroll=8)
        def _(i):
            y = start + i
            pad[y, pl.ds(planes, planes), :] = source[pl.ds(y, planes, stride=rows), :].astype(BF16)

    fetches[0].wait()
    own_rows(est, pad1, 0, rows)

    pl.semaphore_wait(barrier, n - 1 + nv - 1)

    left, right = lax.rem(me + n - 1, n), lax.rem(me + 1, n)

    def neighbours(start_row, count, pad, send_sems, recv_sems, c):
        def copy(side):
            return pltpu.make_async_remote_copy(
                src_ref=pad.at[pl.ds(start_row, count), pl.ds(planes, planes), :],
                dst_ref=pad.at[pl.ds(start_row, count), pl.ds(side * 2 * planes, planes), :],
                send_sem=send_sems.at[side, c],
                recv_sem=recv_sems.at[side, c],
                device_id={"gz": (right, left)[side]},
                device_id_type=pl.DeviceIdType.MESH,
            )

        return copy

    def on_sides(to_right, to_left, arriving=False):
        @pl.when(me > 0 if arriving else me < n - 1)
        def _():
            to_right()

        @pl.when(me < n - 1 if arriving else me > 0)
        def _():
            to_left()

    def share_copy(c):
        return neighbours(mv * share + c * piece, piece, pad1, share_send, share_recv, c)

    def pass_copy(side, c, peer, owner):
        block = pad1.at[pl.ds(owner * share + c * piece, piece), pl.ds(side * 2 * planes, planes), :]
        return pltpu.make_async_remote_copy(
            src_ref=block,
            dst_ref=block,
            send_sem=pass_send.at[peer, side, c],
            recv_sem=pass_recv.at[owner, side, c],
            device_id={"view": peer},
            device_id_type=pl.DeviceIdType.MESH,
        )

    if nv == 2 and lat <= 16 and share > 16:
        lead = (share + 16) // height
        rest = block_rows - lead
        segments = [(d, (1 - mv) * rest, lead) for d in range(height)]
        later = [(d, mv * lead, rest) for d in range(height)]
    else:
        segments = [(d, 0, block_rows) for d in range(height)]
        later = []

    def segment_start(d, at):
        return pl.multiple_of(d * block_rows + at, 8)

    def halo(c):
        d, at, count = (segments + later)[c]
        return neighbours(segment_start(d, at), count, pad2, halo_send, halo_recv, c)

    for c in range(2):
        copy = share_copy(c)
        on_sides(copy(0).start, copy(1).start)

    @pl.when(me == 0)
    def _():
        for pad in (pad1, pad2):
            pad[:, pl.ds(0, planes), :] = jnp.zeros((rows, planes, cols), BF16)

    @pl.when(me == n - 1)
    def _():
        for pad in (pad1, pad2):
            pad[:, pl.ds(2 * planes, planes), :] = jnp.zeros((rows, planes, cols), BF16)

    for fetch in fetches[1:]:
        fetch.wait()
    source = iota((cols, cols), 0)
    low = (1.0 - frac_x[...]).astype(BF16).astype(F32)
    high = frac_x[...].astype(BF16).astype(F32)
    along = jnp.where(source == off_x[...], low, 0.0) + jnp.where(source == off_x[...] + 1, high, 0.0)
    along_b = along.astype(BF16)
    quarter = bricks * cells // 4
    for i in range(4):
        work[i * quarter:(i + 1) * quarter, :] = jnp.dot(
            raw[i * quarter:(i + 1) * quarter, :], along_b, preferred_element_type=F32
        ).astype(BF16).astype(F32)
    for q in range(cells):
        by_cell[:, q * cols:(q + 1) * cols] = work[pl.ds(q, bricks, stride=cells), :].astype(BF16)
    unit = (iota((cols, cols), 0) == iota((cols, cols), 1)).astype(F32)
    for a in range(depth):
        for c in range(depth):
            wz = small_weight(off_z, frac_z, c, a)
            for e in range(height):
                for d in range(height):
                    wy = small_weight(off_y, frac_y, d, e)
                    weights[
                        (a * height + e) * cols:(a * height + e + 1) * cols,
                        (c * height + d) * cols:(c * height + d + 1) * cols,
                    ] = (unit * (wz * wy)).astype(BF16)
    for i in range(wide // 256):
        mixed[:, i * 256:(i + 1) * 256] = jnp.dot(
            by_cell[...], weights[:, i * 256:(i + 1) * 256], preferred_element_type=F32
        ).astype(BF16)

    slab_v = slab[...]
    member = iota((n, bricks), 0) == slab_v
    before = (iota((bricks, bricks), 0) < iota((bricks, bricks), 1)).astype(F32).astype(BF16)
    earlier = jnp.dot(member.astype(F32).astype(BF16), before, preferred_element_type=F32)
    order = jnp.sum(jnp.where(member, earlier, 0.0), axis=0, keepdims=True).astype(jnp.int32)
    slot_scr[...] = slab_v * cap + order
    pos_v = pos[...]
    row16 = iota((16, bricks), 0)
    pos_pair = jnp.where(
        row16 == 0, pos_v // 64 + 1, jnp.where(row16 == 1, lax.rem(pos_v, 64), 0)
    ).astype(F32).astype(BF16)
    for i in range(slots // 256):
        chosen = ((iota((256, bricks), 0) + i * 256) == slot_scr[...]).astype(F32).astype(BF16)
        outgoing[i * 256:(i + 1) * 256, :] = jnp.dot(
            chosen, mixed[...], preferred_element_type=F32
        ).astype(BF16)
        slot_pos = lax.dot_general(
            pos_pair, chosen, (((1,), (1,)), ((), ())), preferred_element_type=F32
        )
        for j in range(256 // cap):
            pos_out[i * (256 // cap) + j, :, 0:cap] = slot_pos[:, j * cap:(j + 1) * cap].astype(BF16)

    def brick_copy(peer, owner):
        return pltpu.make_async_remote_copy(
            src_ref=outgoing.at[pl.ds(pl.multiple_of(peer * cap, cap), cap), :],
            dst_ref=arrived.at[pl.ds(pl.multiple_of(owner * cap, cap), cap), :],
            send_sem=brick_send.at[peer],
            recv_sem=brick_recv.at[owner],
            device_id={"gz": peer},
            device_id_type=pl.DeviceIdType.MESH,
        )

    def pos_copy(peer, owner):
        return pltpu.make_async_remote_copy(
            src_ref=pos_out.at[peer],
            dst_ref=pos_in.at[owner],
            send_sem=pos_send.at[peer],
            recv_sem=pos_recv.at[owner],
            device_id={"gz": peer},
            device_id_type=pl.DeviceIdType.MESH,
        )

    @pl.loop(1, n)
    def _(i):
        pos_copy(lax.rem(me + i, n), me).start()

    by_four = n // 4 if n % 4 == 0 else 0
    orders = [(0, by_four, 4, 2), (0, 2 * by_four, 2, 1), (1, by_four, 4, 0)]
    for begin, end, stride, offset in orders if by_four else [(1, n, 1, 0)]:
        @pl.loop(begin, end)
        def _(i):
            brick_copy(lax.rem(me + i * stride + offset, n), me).start()

    mine = pl.ds(pl.multiple_of(me * cap, cap), cap)
    own_bricks = pltpu.make_async_copy(outgoing.at[mine, :], arrived.at[mine, :], own_sem.at[0])
    own_pos = pltpu.make_async_copy(pos_out.at[me], pos_in.at[me], own_sem.at[1])
    own_bricks.start()
    own_pos.start()

    def true_row(r):
        return lax.rem(r, block_rows) * height + r // block_rows

    ii, jj = iota((rows, rows), 0), iota((rows, rows), 1)
    fy = tap_table(psf_y, taps_l, jj - true_row(ii) + lat)
    back_y[...] = tap_table(psf_y, taps_l, ii - true_row(jj) + lat)
    ci, cj = iota((cols, cols), 0), iota((cols, cols), 1)
    fx = tap_table(psf_x, taps_l, ci - cj + lat)
    x_tables[mv] = tap_table(psf_x, taps_l, cj - ci + lat)
    zi, zj = iota((planes, 3 * planes), 0), iota((planes, 3 * planes), 1)
    fz = tap_table(psf_z, taps_z, zj - zi - (planes - half))
    bz = tap_table(psf_z, taps_z, planes + half + zi - zj)

    def xt_copy(peer, owner):
        return pltpu.make_async_remote_copy(
            src_ref=x_tables.at[mv],
            dst_ref=x_tables.at[owner],
            send_sem=xt_send.at[peer],
            recv_sem=xt_recv.at[owner],
            device_id={"view": peer},
            device_id_type=pl.DeviceIdType.MESH,
        )

    @pl.loop(1, nv)
    def _(i):
        xt_copy(lax.rem(mv + i, nv), mv).start()

    def z_pass(pad, table, start, count):
        @pl.loop(0, count // 4, unroll=2)
        def _(i):
            y = start + i * 4
            block = jnp.concatenate([pad[y + j] for j in range(4)], axis=1)
            result = jnp.dot(table, block, preferred_element_type=F32)
            result = result.astype(BF16).astype(F32)
            for j in range(4):
                work[pl.ds((y + j) * planes, planes), :] = result[:, j * cols:(j + 1) * cols]

    def y_pass(table, z):
        block = jnp.concatenate(
            [work[pl.ds(z + j, rows, stride=planes), :].astype(BF16) for j in range(2)], axis=1
        )
        return jnp.dot(table, block, preferred_element_type=F32).astype(BF16)

    def pass_on(side, c):
        @pl.loop(1, nv)
        def _(i):
            pass_copy(side, c, lax.rem(mv + i, nv), mv).start()

    def pass_take(side, c, owner):
        pass_copy(side, c, mv, owner).wait_recv()

    def pass_sent(side, c):
        @pl.loop(1, nv)
        def _(i):
            pass_copy(side, c, lax.rem(mv + i, nv), mv).wait_send()

    for c in range(2):
        copy = share_copy(c)
        on_sides(copy(0).wait_recv, copy(1).wait_recv, arriving=True)
        on_sides(lambda: pass_on(0, c), lambda: pass_on(1, c), arriving=True)
    z_pass(pad1, fz, mv * share, share)
    for v in range(1, nv):
        owner = lax.rem(mv + nv - v, nv)
        for c in range(2):
            on_sides(lambda: pass_take(0, c, owner), lambda: pass_take(1, c, owner), arriving=True)
            z_pass(pad1, fz, owner * share + c * piece, piece)

    @pl.loop(0, planes // 2, unroll=4)
    def _(i):
        along_y = y_pass(fy, 2 * i)
        for j in range(2):
            inverse[2 * i + j] = 1.0 / jnp.dot(
                along_y[:, j * cols:(j + 1) * cols], fx, preferred_element_type=F32
            )

    own_pos.wait()

    @pl.loop(1, n)
    def _(i):
        pos_copy(me, lax.rem(me + n - i, n)).wait_recv()

    for s in range(n):
        pair = pos_in[s].astype(F32)
        pos_row[0:1, s * cap:(s + 1) * cap] = ((pair[0:1] - 1.0) * 64.0 + pair[1:2])[:, 0:cap]
    for i in range(places // 128):
        place = (iota((128, slots), 0) + i * 128).astype(F32)
        placer[i * 128:(i + 1) * 128, :] = (place == pos_row[0:1, :]).astype(F32).astype(BF16)

    own_bricks.wait()

    @pl.loop(1, n)
    def _(i):
        brick_copy(me, lax.rem(me + n - i, n)).wait_recv()

    for c in range(depth):
        for d in range(height):
            at = (c * height + d) * cols
            if d % 2 == 0:
                added = jnp.dot(placer[...], arrived[:, at:at + 2 * cols], preferred_element_type=F32)
            joined[:, c, d, :, :] = added[:, (d % 2) * cols:(d % 2 + 1) * cols].reshape(
                block_planes, block_rows, cols
            )

    for c, (d, at, count) in enumerate(segments + later):
        start = segment_start(d, at)

        @pl.loop(0, block_planes)
        def _(i):
            for k in range(depth):
                z = i * depth + k
                work[pl.ds(pl.multiple_of(z * rows + start, 8), count), :] = (
                    1.0 + joined[i, k, d, pl.ds(pl.multiple_of(at, 8), count), :]
                ) * inverse[z, pl.ds(start, count), :]

        own_rows(work, pad2, start, count)
        copy = halo(c)
        on_sides(copy(0).start, copy(1).start)

    def arrive(c):
        d, at, count = (segments + later)[c]
        copy = halo(c)
        on_sides(copy(0).wait_recv, copy(1).wait_recv, arriving=True)
        z_pass(pad2, bz, segment_start(d, at), count)

    def back_rows(view, z):
        at = pl.multiple_of(view * share, share)
        along_y = y_pass(back_y[pl.ds(at, share), :], z)
        for j in range(2):
            back[z + j, pl.ds(at, share), :] = along_y[:, j * cols:(j + 1) * cols]

    for c in range(len(segments)):
        arrive(c)

    def view_copy(peer, owner, c):
        return pltpu.make_async_remote_copy(
            src_ref=back.at[pl.ds(c * zpart, zpart), pl.ds(pl.multiple_of(peer * share, share), share), :],
            dst_ref=from_views.at[owner, pl.ds(c * zpart, zpart), :, :],
            send_sem=view_send.at[peer, c],
            recv_sem=view_recv.at[owner, c],
            device_id={"view": peer},
            device_id_type=pl.DeviceIdType.MESH,
        )

    for c in range(CHUNKS):
        for v in range(1, nv):
            peer = lax.rem(mv + v, nv)

            @pl.loop(0, zpart // 2, unroll=4)
            def _(i):
                back_rows(peer, c * zpart + 2 * i)

            view_copy(peer, mv, c).start()

    for c in range(len(later)):
        arrive(len(segments) + c)

    @pl.loop(0, planes // 2, unroll=4)
    def _(i):
        back_rows(mv, 2 * i)

    first = pl.multiple_of(mv * share, share)

    @pl.loop(1, nv)
    def _(i):
        xt_copy(mv, lax.rem(mv + i, nv)).wait_recv()

    for c in range(CHUNKS):
        @pl.loop(1, nv)
        def _(i):
            view_copy(mv, lax.rem(mv + i, nv), c).wait_recv()

        planes_c = slice(c * zpart, (c + 1) * zpart)
        total = jnp.dot(
            back[planes_c, pl.ds(first, share), :].reshape(zpart * share, cols),
            x_tables[mv],
            preferred_element_type=F32,
        )
        for v in range(1, nv):
            other = lax.rem(mv + v, nv)
            total = total + jnp.dot(
                from_views[other, planes_c].reshape(zpart * share, cols),
                x_tables[other],
                preferred_element_type=F32,
            )
        for k in range(zpart):
            z = c * zpart + k
            out[z] = (
                est[pl.ds(pl.multiple_of(z * rows + first, share), share), :]
                * total[k * share:(k + 1) * share]
                * (1.0 / nv)
            )

    for c in range(2):
        copy = share_copy(c)
        on_sides(copy(0).wait_send, copy(1).wait_send)
        on_sides(lambda: pass_sent(0, c), lambda: pass_sent(1, c), arriving=True)
    for c in range(len(segments + later)):
        copy = halo(c)
        on_sides(copy(0).wait_send, copy(1).wait_send)
    for c in range(CHUNKS):
        @pl.loop(1, nv)
        def _(i):
            view_copy(lax.rem(mv + i, nv), mv, c).wait_send()

    @pl.loop(1, nv)
    def _(i):
        xt_copy(lax.rem(mv + i, nv), mv).wait_send()

    @pl.loop(1, n)
    def _(i):
        peer = lax.rem(me + i, n)
        brick_copy(peer, me).wait_send()
        pos_copy(peer, me).wait_send()


def shards(
    estimate, raw_bricks, brick_slab, brick_pos, off_z, frac_z, off_y, frac_y, off_x, frac_x,
    psf_z, psf_y, psf_x,
):
    planes, rows, cols = estimate.shape
    _, bricks, depth, height, _ = raw_bricks.shape
    n, nv = lax.axis_size("gz"), lax.axis_size("view")
    taps_z, taps_l = psf_z.shape[1], psf_x.shape[1]
    cells = depth * height
    wide = cells * cols
    cap = max(2, 2 * bricks // n)
    slots = n * cap
    share = rows // nv
    block_planes, block_rows = planes // depth, rows // height
    places = block_planes * block_rows
    dims = (planes, rows, cols, depth, height, bricks, n, nv, taps_z, taps_l)
    vmem = pl.BlockSpec(memory_space=pltpu.VMEM)
    dma = pltpu.SemaphoreType.DMA
    operands = (
        estimate.reshape(planes * rows, cols),
        raw_bricks.reshape(bricks * cells, cols),
        brick_slab.reshape(1, bricks),
        brick_pos,
        off_z, frac_z, off_y, frac_y, off_x, frac_x, psf_z, psf_y, psf_x,
    )
    return pl.pallas_call(
        functools.partial(step, dims),
        out_shape=jax.ShapeDtypeStruct((planes, share, cols), F32),
        in_specs=[pl.BlockSpec(memory_space=pltpu.HBM)] * 13,
        out_specs=vmem,
        scratch_shapes=[pltpu.VMEM(o.shape, o.dtype) for o in operands] + [
            dma((13,)),
            pltpu.VMEM((rows, 3 * planes, cols), BF16),
            pltpu.VMEM((rows, 3 * planes, cols), BF16),
            pltpu.VMEM((max(rows * planes, bricks * cells), cols), F32),
            pltpu.VMEM((planes, rows, cols), F32),
            pltpu.VMEM((block_planes, depth, height, block_rows, cols), F32),
            pltpu.VMEM((wide, wide), BF16),
            pltpu.VMEM((bricks, wide), BF16),
            pltpu.VMEM((bricks, wide), BF16),
            pltpu.VMEM((slots, wide), BF16),
            pltpu.VMEM((slots, wide), BF16),
            pltpu.VMEM((n, 16, 128), BF16),
            pltpu.VMEM((n, 16, 128), BF16),
            pltpu.VMEM((8, slots), F32),
            pltpu.VMEM((places, slots), BF16),
            pltpu.VMEM((rows, rows), BF16),
            pltpu.VMEM((planes, rows, cols), BF16),
            pltpu.VMEM((nv, planes, share, cols), BF16),
            pltpu.VMEM((nv, cols, cols), BF16),
            pltpu.VMEM((1, bricks), jnp.int32),
            dma((2, 2 * height)),
            dma((2, 2 * height)),
            dma((2, 2)),
            dma((2, 2)),
            dma((nv, 2, 2)),
            dma((nv, 2, 2)),
            dma((n,)),
            dma((n,)),
            dma((n,)),
            dma((n,)),
            dma((nv, CHUNKS)),
            dma((nv, CHUNKS)),
            dma((nv,)),
            dma((nv,)),
            dma((2,)),
        ],
        compiler_params=pltpu.CompilerParams(
            collective_id=0, has_side_effects=True, vmem_limit_bytes=63 * 1024 * 1024
        ),
    )(*operands)


def solution(mesh):
    in_specs = (
        P("gz", None, None),
        P("view", "gz", None, None, None),
        P("view", "gz", None),
        P("view", "gz"),
    ) + (P("view", None),) * 9
    out_specs = P("gz", "view", None)
    return jax.shard_map(shards, mesh=mesh, in_specs=in_specs, out_specs=out_specs, check_vma=False)
```
